32 devices in a mesh: dom: 16 (over z, y, core), col: 2 (over x).
Axes of the slice: x: 2, y: 2, z: 4, core: 2. Of those that a mesh axis runs over, the one named last changes fastest.
Arguments:
- features: bfloat16 [128, 4096], P('col', 'dom'), may hold values from -6 to 6
- cached_embed: bfloat16 [128, 4096], P('col'), may hold values from -6 to 6
- staleness: int32 [16], replicated, may hold values from 0 to 15, as said below
- node_counts: int32 [16], replicated, may hold values from 64 to 256, as said below
- neighbours: int32 [16, 4096], P(None, 'dom'), may hold values from 0 to 4095, as said below
- degrees: int32 [4096], P('dom'), may hold values from 1 to 16
- w_self: bfloat16 [128, 256], P('col'), may hold values from -0.5 to 0.5
- w_nbr: bfloat16 [128, 256], P('col'), may hold values from -0.5 to 0.5
- sage_bias: float32 [256], P('col'), may hold values from -3 to 3
- cotangent: bfloat16 [256, 4096], P('col', 'dom'), may hold values from -6 to 6
Outputs:
- activation: bfloat16 [256, 4096], P('col', 'dom')
- grad_feat: bfloat16 [128, 4096], P('col', 'dom')
- grad_self: float32 [128, 256], P('col')
- grad_nbr: float32 [128, 256], P('col')
- grad_bias: float32 [256], P('col')
The draws below stay inside these ranges and needn't reach their ends.
Inputs may be any that keep to these rules, and one draw needn't show every extreme that they name: Exactly 4 partitions have staleness of 8 or more. `node_counts`: some partition has all 256 node slots live. `neighbours`: every neighbour slot names a live node slot; about half lie in the node's own partition.
All inputs are finite; a program needn't handle non-finite values.
Results may differ from the reference program's by a relative error of at most 0.015.
Values may be sent and summed in bfloat16 or wider, within the bound.
No kernel may reach another device: no remote copies, remote signals or barrier semaphores. Data moves between devices by JAX's collectives and lax.ppermute only.
A program may use at most 64 MiB of HBM per device.

```python
import jax
import jax.numpy as jnp

F = 128
H = 256
K = 16
LIMIT = 8
P_DEV = 256
PARTS_SIZE = 16
NODES = 4096
FRESH = 4


def graph_counts(key):
    count_key = jax.random.fold_in(key, 11)
    values = jax.random.randint(jax.random.fold_in(count_key, 1), (PARTS_SIZE,), P_DEV // 4, P_DEV + 1)
    chosen = jax.random.randint(jax.random.fold_in(count_key, 2), (), 0, PARTS_SIZE)
    return values.at[chosen].set(P_DEV).astype(jnp.int32)


def draw_node_counts(key, part):
    return graph_counts(key)


def draw_neighbours(key, part):
    counts = graph_counts(key)
    nbr_key = jax.random.fold_in(key, 23)
    own_part = (jnp.arange(NODES, dtype=jnp.int32) // P_DEV)[:, None] + jnp.zeros((NODES, K), jnp.int32)
    other_part = jax.random.randint(jax.random.fold_in(nbr_key, 1), (NODES, K), 0, PARTS_SIZE)
    picker = jax.random.randint(jax.random.fold_in(nbr_key, 2), (NODES, K), 0, 2)
    source_part = jnp.where(picker == 1, own_part, other_part)
    offset = jax.random.randint(jax.random.fold_in(nbr_key, 3), (NODES, K), 0, 1 << 20) % counts[source_part]
    return (source_part * P_DEV + offset).astype(jnp.int32).T


def draw_degrees(key, part):
    values = jax.random.randint(jax.random.fold_in(key, 37), (NODES,), 1, K + 1)
    return values.at[0].set(K).astype(jnp.int32)


def draw_staleness(key, part):
    order_key = jax.random.fold_in(key, 41)
    shuffled = jax.random.permutation(jax.random.fold_in(order_key, 1), PARTS_SIZE)
    rank_pos = jnp.arange(PARTS_SIZE, dtype=jnp.int32)
    low_vals = jax.random.randint(jax.random.fold_in(order_key, 2), (PARTS_SIZE,), 0, LIMIT)
    values = jnp.where(rank_pos < FRESH, low_vals + LIMIT, low_vals)
    values = jnp.where(rank_pos == 0, 2 * LIMIT - 1, values)
    values = jnp.where(rank_pos == FRESH, 0, values)
    return jnp.zeros((PARTS_SIZE,), jnp.int32).at[shuffled].set(values.astype(jnp.int32))


def block_scale(key, dims, split, smallest, largest):
    def one(position, blocks):
        steps = jax.random.uniform(jax.random.fold_in(jax.random.fold_in(key, 6), position), (blocks,), jnp.float32, smallest / len(split), largest / len(split))
        return jnp.repeat(jnp.exp(steps), dims[position] // blocks).reshape((-1,) + (1,) * (len(dims) - position - 1))

    gain = one(*split[0])
    for cut in split[1:]:
        gain = gain * one(*cut)
    return gain


def noise(stream_key, shape, deviation, most, shards=(), kind=jnp.bfloat16):
    values = jax.random.normal(stream_key, shape, jnp.float32) * deviation
    if len(shards) > 0:
        values = block_scale(stream_key, shape, shards, -0.22, 0.18) * values
    return jnp.clip(values, min=-most, max=most).astype(kind)


def setup_inputs(seed: int = 0) -> dict:
    streams_of = jax.random.split(jax.random.key(seed), 11)
    features = noise(streams_of[0], (F, NODES), 1.0, 6.0, ((0, 2), (1, 16)))
    cached_embed = noise(streams_of[1], (F, NODES), 1.0, 6.0, ((0, 2),))
    staleness = draw_staleness(jax.random.fold_in(streams_of[10], 71), 0)
    node_counts = draw_node_counts(jax.random.fold_in(streams_of[10], 71), 0)
    neighbours = draw_neighbours(jax.random.fold_in(streams_of[10], 71), 0)
    degrees = draw_degrees(jax.random.fold_in(streams_of[10], 71), 0)
    w_self = noise(streams_of[6], (F, H), F ** -0.5, 0.5, ((0, 2),))
    w_nbr = noise(streams_of[7], (F, H), F ** -0.5, 0.5, ((0, 2),))
    sage_bias = noise(streams_of[8], (H,), 0.5, 3.0, ((0, 2),), jnp.float32)
    cotangent = noise(streams_of[9], (H, NODES), 1.0, 6.0, ((0, 2), (1, 16)))
    return dict(features=features, cached_embed=cached_embed, staleness=staleness, node_counts=node_counts, neighbours=neighbours, degrees=degrees, w_self=w_self, w_nbr=w_nbr, sage_bias=sage_bias, cotangent=cotangent)


def reference(features, cached_embed, staleness, node_counts, neighbours, degrees, w_self, w_nbr, sage_bias, cotangent):
    feat_rows = features.T
    cache_rows = cached_embed.T
    nbr_rows = neighbours.T
    cot_rows = cotangent.T
    node_slot = jnp.arange(NODES, dtype=jnp.int32)
    part_of = node_slot // P_DEV
    fresh_flag = (staleness >= LIMIT).astype(jnp.int32)
    fresh_rows = fresh_flag[part_of]
    sources = jnp.where(fresh_rows[:, None] == 1, feat_rows, cache_rows)
    live_rows = (node_slot % P_DEV < node_counts[part_of]).astype(jnp.float32)
    slot_index = jnp.arange(K, dtype=jnp.int32)
    used = (slot_index[None, :] < degrees[:, None]).astype(jnp.float32)
    weights = used * (live_rows / degrees.astype(jnp.float32))[:, None]
    gathered = sources[nbr_rows].astype(jnp.float32)
    aggregated = jnp.einsum("nk,nkc->nc", weights, gathered).astype(jnp.bfloat16)
    pre_act = (jnp.dot(feat_rows, w_self, preferred_element_type=jnp.float32)
               + jnp.dot(aggregated, w_nbr, preferred_element_type=jnp.float32) + sage_bias)
    sigmoid = 1.0 / (1.0 + jnp.exp(-pre_act))
    activation = (live_rows[:, None] * pre_act * sigmoid).astype(jnp.bfloat16)
    grad_pre = (live_rows[:, None] * cot_rows.astype(jnp.float32) * sigmoid * (1.0 + pre_act * (1.0 - sigmoid))).astype(jnp.bfloat16)
    grad_bias = jnp.sum(grad_pre.astype(jnp.float32), axis=0)
    grad_self = jnp.dot(feat_rows.T, grad_pre, preferred_element_type=jnp.float32)
    grad_nbr = jnp.dot(aggregated.T, grad_pre, preferred_element_type=jnp.float32)
    grad_agg = jnp.dot(grad_pre, w_nbr.T, preferred_element_type=jnp.float32).astype(jnp.bfloat16)
    own_term = jnp.dot(grad_pre, w_self.T, preferred_element_type=jnp.float32)
    spread = weights[:, :, None] * grad_agg.astype(jnp.float32)[:, None, :]
    back = jnp.zeros((NODES, F), jnp.float32).at[nbr_rows.reshape(-1)].add(spread.reshape(-1, F))
    grad_feat = (own_term + fresh_rows.astype(jnp.float32)[:, None] * back).astype(jnp.bfloat16)
    return activation.T, grad_feat.T, grad_self, grad_nbr, grad_bias
```

```python
import functools

import jax
import jax.numpy as jnp
from jax import lax
from jax.experimental import pallas as pl
from jax.experimental.pallas import tpu as pltpu
from jax.sharding import PartitionSpec as P

LIMIT = 8
LANES = 128
BF16 = jnp.bfloat16
F32 = jnp.float32
SMEM = pl.BlockSpec(memory_space=pltpu.SMEM)
VMEM = pl.BlockSpec(memory_space=pltpu.VMEM)
PARAMS = pltpu.CompilerParams(vmem_limit_bytes=32 * 1024 * 1024)


def call(body, outs, smem_count, vmem_count, scratch=(), flops=0, moved=0, **kw):
    return pl.pallas_call(
        body,
        out_shape=outs,
        in_specs=[SMEM] * smem_count + [VMEM] * vmem_count,
        out_specs=jax.tree.map(lambda _: VMEM, outs),
        scratch_shapes=list(scratch),
        compiler_params=PARAMS,
        cost_estimate=pl.CostEstimate(flops=flops, bytes_accessed=moved, transcendentals=0),
        **kw,
    )


def count_body(stale_ref, nbr_ref, deg_ref, cache_ref, listed_ref, acc_ref, all_ref):
    slots, nodes = nbr_ref.shape
    parts = stale_ref.shape[0]
    listed = listed_ref.shape[0] // nodes
    used = lax.broadcasted_iota(jnp.int32, (slots, nodes), 0) < deg_ref[...]
    index = jnp.where(used, nbr_ref[...], -1)
    tall = 32

    def per_rows(step, carry):
        top = pl.multiple_of(step * tall, tall)
        place = lax.broadcasted_iota(jnp.int32, (tall, nodes), 0) + top
        total = jnp.zeros((tall, nodes), F32)
        for k in range(slots):
            total = total + jnp.where(index[k : k + 1, :] == place, F32(1), F32(0))
        all_ref[pl.ds(top, tall), :] = total.astype(BF16)
        return carry

    lax.fori_loop(0, parts * nodes // tall, per_rows, jnp.int32(0))

    def per_part(part, rank):
        fresh = stale_ref[part] >= LIMIT
        rows = pl.ds(pl.multiple_of(part * nodes, nodes), nodes)

        @pl.when(fresh)
        def _():
            to = pl.multiple_of(jnp.minimum(rank, listed - 1) * nodes, nodes)
            listed_ref[pl.ds(to, nodes), :] = all_ref[rows, :]
            all_ref[rows, :] = jnp.zeros((nodes, nodes), BF16)

        return rank + fresh.astype(jnp.int32)

    lax.fori_loop(0, parts, per_part, jnp.int32(0))
    acc_ref[...] = jnp.dot(cache_ref[...], all_ref[...], preferred_element_type=F32)


def fold_body(x_ref, out_ref):
    width, nodes = x_ref.shape
    for h in range(nodes // LANES):
        out_ref[h * width : (h + 1) * width, :] = x_ref[:, h * LANES : (h + 1) * LANES]


def pick_body(stale_ref, got_ref, out_ref, wide, kept):
    parts = stale_ref.shape[0]
    tall = got_ref.shape[0] // parts
    listed = kept.shape[0] // tall
    wide[...] = got_ref[...].astype(F32)

    def per_part(part, rank):
        fresh = stale_ref[part] >= LIMIT

        @pl.when(fresh)
        def _():
            row = pl.multiple_of(jnp.minimum(rank, listed - 1) * tall, tall)
            kept[pl.ds(row, tall), :] = wide[pl.ds(pl.multiple_of(part * tall, tall), tall), :]

        return rank + fresh.astype(jnp.int32)

    lax.fori_loop(0, parts, per_part, jnp.int32(0))
    slot = kept[...].astype(BF16)
    for d in range(out_ref.shape[0]):
        out_ref[d] = slot


def node_weights(counts_ref, deg):
    nodes = deg.shape[1]
    live = (
        lax.broadcasted_iota(jnp.int32, (1, nodes), 1) < counts_ref[lax.axis_index("dom")]
    ).astype(F32)
    return live, live / deg.astype(F32)


def mean_body(counts_ref, deg_ref, acc_ref, fresh_ref, listed_ref, out_ref):
    width, nodes = acc_ref.shape
    listed = listed_ref.shape[0] // nodes
    chunks, tall = fresh_ref.shape[0], fresh_ref.shape[1] // listed
    halves = nodes // LANES
    groups = chunks // halves
    total = acc_ref[...]
    fresh = fresh_ref[...].astype(F32).reshape(chunks, listed, tall, LANES)
    for r in range(listed):
        for h in range(halves):
            piece = fresh[h * groups : (h + 1) * groups, r].reshape(width, LANES).astype(BF16)
            row = r * nodes + h * LANES
            total += jnp.dot(piece, listed_ref[row : row + LANES, :], preferred_element_type=F32)
    _, weight = node_weights(counts_ref, deg_ref[...])
    out_ref[...] = (total * weight).astype(BF16)


def dense_body(n_col, dom, counts_ref, deg_ref, listed_ref, *refs):
    ins = refs[: 6 * n_col]
    act_ref, own_ref, slot_ref, cot_full, bias_full, full = refs[6 * n_col :]
    feats, aggs, selfs, nbrs, biases, cots = [ins[i * n_col : (i + 1) * n_col] for i in range(6)]
    width, nodes = feats[0].shape
    part_h = cots[0].shape[0]
    me = lax.axis_index("col")
    live, weight = node_weights(counts_ref, deg_ref[...])
    pre = jnp.zeros((part_h * n_col, nodes), F32)
    for s in range(n_col):
        rows = pl.ds(pl.multiple_of(lax.rem(me + n_col - s, n_col) * part_h, part_h), part_h)
        cot_full[rows, :] = cots[s][...].astype(F32)
        bias_full[rows, :] = jnp.broadcast_to(biases[s][...], (LANES, part_h)).T
        for w, x in ((selfs[s], feats[s]), (nbrs[s], aggs[s])):
            pre += jnp.dot(w[...].astype(F32).T.astype(BF16), x[...], preferred_element_type=F32)
    pre += jnp.concatenate([bias_full[...]] * (nodes // LANES), 1)
    sig = 1.0 / (1.0 + jnp.exp(-pre))
    full[...] = live * pre * sig
    own_rows = pl.ds(pl.multiple_of(me * part_h, part_h), part_h)
    act_ref[...] = full[own_rows, :].astype(BF16)
    grad = (live * cot_full[...] * sig * (1.0 + pre * (1.0 - sig))).astype(BF16)
    cot_full[...] = grad.astype(F32)
    back = jnp.dot(nbrs[0][...], grad, preferred_element_type=F32)
    own_ref[...] = jnp.dot(selfs[0][...], grad, preferred_element_type=F32)
    spread = (weight * back.astype(BF16).astype(F32)).astype(BF16)
    contrib = lax.dot_general(
        spread, listed_ref[...], (((1,), (1,)), ((), ())), preferred_element_type=F32
    )
    wgrads = [
        lax.dot_general(x[...], grad, (((1,), (1,)), ((), ())), preferred_element_type=F32)
        for x in (feats[0], aggs[0])
    ]
    ones = jnp.ones((16, nodes), BF16)
    bias = lax.dot_general(
        ones, cot_full[own_rows, :].astype(BF16), (((1,), (1,)), ((), ())), preferred_element_type=F32
    )[:8]
    high = bias.astype(BF16).astype(F32)
    listed = listed_ref.shape[0] // nodes
    halves = nodes // LANES
    hidden = part_h * n_col
    for d in range(dom):
        s, h = d // halves, d % halves
        pieces = [
            contrib[8 * s : 8 * s + 8, r * nodes + h * LANES : r * nodes + (h + 1) * LANES]
            for r in range(listed)
        ]
        which, row = divmod(8 * d, width)
        pieces += [
            wgrads[which][row : row + 8, i * LANES : (i + 1) * LANES] for i in range(hidden // LANES)
        ]
        slot_ref[d] = jnp.concatenate(pieces + [high, bias - high], 0).astype(BF16)


def total_body(stale_ref, got_ref, out_ref, bias_ref, kept):
    dom = got_ref.shape[0]
    listed = stale_ref.shape[0] // 4
    total = got_ref[0].astype(F32)
    for d in range(1, dom):
        total += got_ref[d].astype(F32)
    split = 8 * listed
    kept[...] = total[:split]
    weight = total[split : split + 16]
    bias_ref[...] = total[split + 16 : split + 24][:1] + total[split + 24 :][:1]

    def per_part(part, rank):
        mine = kept[pl.ds(pl.multiple_of(jnp.minimum(rank, listed - 1) * 8, 8), 8), :]
        out_ref[part] = jnp.concatenate([weight, mine, jnp.zeros_like(mine)], 0).astype(BF16)
        return rank + (stale_ref[part] >= LIMIT).astype(jnp.int32)

    lax.fori_loop(0, dom, per_part, jnp.int32(0))


def last_body(stale_ref, own_ref, got_ref, feat_ref, self_ref, nbr_ref):
    width, nodes = own_ref.shape
    fresh = (stale_ref[lax.axis_index("dom")] >= LIMIT).astype(F32)
    dom = got_ref.shape[0]
    halves = nodes // LANES
    for s in range(width // 16):
        rows = []
        for g in (2 * s, 2 * s + 1):
            rows.append(
                jnp.concatenate([got_ref[g * halves + h, 16:32].astype(F32)[:8] for h in range(halves)], 1)
            )
        span = slice(16 * s, 16 * s + 16)
        feat_ref[span, :] = (own_ref[span, :] + fresh * jnp.concatenate(rows, 0)).astype(BF16)
    for d in range(dom):
        part = got_ref[d, :16].astype(F32)
        row = jnp.concatenate([part[:8], part[8:]], 1)
        ref, at = (self_ref, d) if 8 * d < width else (nbr_ref, d - width // 8)
        ref[8 * at : 8 * at + 8, :] = row


def per_device(
    n_col,
    features,
    cached_embed,
    staleness,
    node_counts,
    neighbours,
    degrees,
    w_self,
    w_nbr,
    sage_bias,
    cotangent,
):
    width, nodes = features.shape
    hidden = w_self.shape[1]
    dom = staleness.shape[0]
    if width * nodes != dom * 8 * LANES or cotangent.shape[0] != LANES:
        return plain(
            features, cached_embed, staleness, node_counts, neighbours, degrees, w_self, w_nbr, sage_bias, cotangent
        )
    listed = dom // 4
    part_h = cotangent.shape[0]
    shape = jax.ShapeDtypeStruct

    def around(block):
        got = [block]
        for shift in range(1, n_col):
            got.append(
                lax.ppermute(block, "col", [(i, (i + shift) % n_col) for i in range(n_col)])
            )
        return got

    def exchange(slots):
        return lax.all_to_all(slots, "dom", split_axis=0, concat_axis=0, tiled=True)

    halves = nodes // LANES
    chunks = call(fold_body, shape((width * halves, LANES), BF16), 0, 1, moved=4 * features.size)(features)
    got = exchange(chunks.reshape(dom, width * halves // dom, LANES))
    feats, selfs, nbrs = around(features), around(w_self), around(w_nbr)
    biases, cots = around(sage_bias.reshape(1, part_h)), around(cotangent)
    deg = degrees.reshape(1, nodes)
    counts, acc = call(
        count_body,
        (shape((listed * nodes, nodes), BF16), shape((width, nodes), F32)),
        1,
        3,
        [pltpu.VMEM((dom * nodes, nodes), BF16)],
        flops=2 * width * dom * nodes * nodes,
        moved=2 * (dom * nodes * width + listed * nodes * nodes),
    )(staleness, neighbours, deg, cached_embed)
    tall = width * halves // dom
    picked = call(
        pick_body,
        shape((dom, listed * tall, LANES), BF16),
        1,
        1,
        [pltpu.VMEM((dom * tall, LANES), F32), pltpu.VMEM((listed * tall, LANES), F32)],
        moved=4 * got.size,
    )(staleness, got.reshape(dom * tall, LANES))
    fresh = exchange(picked)
    agg = call(mean_body, shape((width, nodes), BF16), 1, 4, moved=2 * fresh.size)(
        node_counts, deg, acc, fresh, counts
    )
    aggs = around(agg)
    rows = 8 * listed + 8 * hidden // LANES + 16
    act, own, slots = call(
        functools.partial(dense_body, n_col, dom),
        (shape((part_h, nodes), BF16), shape((width, nodes), F32), shape((dom, rows, LANES), BF16)),
        1,
        2 + 6 * n_col,
        [pltpu.VMEM((hidden, nodes), F32), pltpu.VMEM((hidden, LANES), F32), pltpu.VMEM((hidden, nodes), F32)],
        flops=2 * width * nodes * (hidden * 6 + listed * nodes),
        moved=4 * dom * rows * LANES,
    )(node_counts, deg, counts, *feats, *aggs, *selfs, *nbrs, *biases, *cots)
    parts = exchange(slots)
    back, bias = call(
        total_body,
        (shape((dom, 32, LANES), BF16), shape((1, LANES), F32)),
        1,
        1,
        [pltpu.VMEM((8 * listed, LANES), F32)],
        moved=4 * parts.size,
    )(staleness, parts)
    final = exchange(back)
    grad_feat, grad_self, grad_nbr = call(
        last_body,
        (shape((width, nodes), BF16), shape((width, hidden), F32), shape((width, hidden), F32)),
        1,
        2,
        moved=4 * final.size,
    )(staleness, own, final)
    return act, grad_feat, grad_self, grad_nbr, bias.reshape(-1)


def left_product(weight, data):
    return lax.dot_general(
        weight, data, (((0,), (0,)), ((), ())), preferred_element_type=jnp.float32
    )


def right_product(data, grads):
    return lax.dot_general(
        data, grads, (((1,), (1,)), ((), ())), preferred_element_type=jnp.float32
    )


def plain(
    features,
    cached_embed,
    staleness,
    node_counts,
    neighbours,
    degrees,
    w_self,
    w_nbr,
    sage_bias,
    cotangent,
):
    col_width = features.shape[0]
    part_rows = features.shape[1]
    slot_count = neighbours.shape[0]
    my_index = lax.axis_index("dom")
    fresh_flag = (staleness >= LIMIT).astype(jnp.int32)
    my_fresh = fresh_flag[my_index]
    own_cache = lax.dynamic_slice_in_dim(cached_embed, my_index * part_rows, part_rows, 1)
    own_source = jnp.where(my_fresh == 1, features, own_cache)
    sources = lax.all_gather(own_source, "dom", axis=1, tiled=True)
    local_slot = jnp.arange(part_rows, dtype=jnp.int32)
    live_rows = (local_slot < node_counts[my_index]).astype(jnp.float32)
    slot_index = jnp.arange(slot_count, dtype=jnp.int32)
    used = (slot_index[:, None] < degrees[None, :]).astype(jnp.float32)
    weights = used * (live_rows / degrees.astype(jnp.float32))[None, :]
    gathered = sources[:, neighbours].astype(jnp.float32)
    aggregated = jnp.sum(weights[None, :, :] * gathered, axis=1).astype(jnp.bfloat16)
    partial_pre = left_product(w_self, features) + left_product(w_nbr, aggregated)
    pre_act = (
        lax.psum_scatter(
            partial_pre.astype(jnp.bfloat16), "col", scatter_dimension=0, tiled=True
        ).astype(jnp.float32)
        + sage_bias[:, None]
    )
    sigmoid = 1.0 / (1.0 + jnp.exp(-pre_act))
    activation = (live_rows[None, :] * pre_act * sigmoid).astype(jnp.bfloat16)
    grad_pre = (
        live_rows[None, :]
        * cotangent.astype(jnp.float32)
        * sigmoid
        * (1.0 + pre_act * (1.0 - sigmoid))
    ).astype(jnp.bfloat16)
    grad_full = lax.all_gather(grad_pre, "col", axis=0, tiled=True)
    self_part = right_product(features, grad_full)
    nbr_part = right_product(aggregated, grad_full)
    bias_part = jnp.sum(grad_pre.astype(jnp.float32), axis=1)
    grad_self, grad_nbr, grad_bias = lax.psum((self_part, nbr_part, bias_part), "dom")
    grad_agg = jnp.dot(w_nbr, grad_full, preferred_element_type=jnp.float32).astype(jnp.bfloat16)
    own_term = jnp.dot(w_self, grad_full, preferred_element_type=jnp.float32)
    spread = weights[None, :, :] * grad_agg.astype(jnp.float32)[:, None, :]
    total_rows = cached_embed.shape[1]
    contrib = (
        jnp.zeros((col_width, total_rows), jnp.float32)
        .at[:, neighbours.reshape(-1)]
        .add(spread.reshape(col_width, -1))
    )
    part_total = lax.axis_size("dom")
    listed_total = part_total // 4
    listed_order = jnp.argsort(1 - fresh_flag, stable=True)[:listed_total]
    blocks = contrib.reshape(col_width, part_total, part_rows)
    kept = jnp.take(blocks, listed_order, axis=1)
    summed = lax.psum(kept, "dom")
    part_ids = jnp.arange(part_total, dtype=jnp.int32)
    my_rank = jnp.sum(jnp.where(part_ids < my_index, fresh_flag, 0))
    my_rank = jnp.minimum(my_rank, listed_total - 1)
    back = lax.dynamic_index_in_dim(summed, my_rank, 1, keepdims=False)
    grad_feat = (own_term + my_fresh.astype(jnp.float32) * back).astype(jnp.bfloat16)
    return (activation, grad_feat, grad_self, grad_nbr, grad_bias)


def solution(mesh):
    placed = (
        P("col", "dom"),
        P("col", None),
        P(),
        P(),
        P(None, "dom"),
        P("dom"),
        P("col", None),
        P("col", None),
        P("col"),
        P("col", "dom"),
    )
    return jax.shard_map(
        functools.partial(per_device, mesh.shape["col"]),
        mesh=mesh,
        in_specs=placed,
        out_specs=(P("col", "dom"), P("col", "dom"), P("col", None), P("col", None), P("col")),
        check_vma=False,
    )
```

```python
import functools

import jax
import jax.numpy as jnp
from jax import lax
from jax.experimental import pallas as pl
from jax.experimental.pallas import tpu as pltpu
from jax.sharding import PartitionSpec as P

LIMIT = 8
LANES = 128
LOW = 4
BF16 = jnp.bfloat16
F32 = jnp.float32
SMEM = pl.BlockSpec(memory_space=pltpu.SMEM)
VMEM = pl.BlockSpec(memory_space=pltpu.VMEM)
PARAMS = pltpu.CompilerParams(vmem_limit_bytes=32 * 1024 * 1024)


def call(body, outs, smem_count, vmem_count, scratch=(), flops=0, moved=0):
    return pl.pallas_call(
        body,
        out_shape=outs,
        in_specs=[SMEM] * smem_count + [VMEM] * vmem_count,
        out_specs=jax.tree.map(lambda _: VMEM, outs),
        scratch_shapes=list(scratch),
        compiler_params=PARAMS,
        cost_estimate=pl.CostEstimate(flops=flops, bytes_accessed=moved, transcendentals=0),
    )


def up16(rows):
    return -(-rows // 16) * 16


def is_fresh(stale_ref, part):
    return stale_ref[part] >= LIMIT


def rank_of(stale_ref, part):
    ahead = lax.fori_loop(
        0, part, lambda p, r: r + is_fresh(stale_ref, p).astype(jnp.int32), jnp.int32(0)
    )
    return jnp.minimum(ahead, stale_ref.shape[0] // 4 - 1)


def split3(x):
    high = x.astype(BF16).astype(F32)
    mid = (x - high).astype(BF16).astype(F32)
    return high, mid, x - high - mid


def count_body(start, total_parts, stale_ref, nbr_ref, deg_ref, cache_ref, *refs):
    slots, nodes = nbr_ref.shape
    *before, listed_ref, acc_ref, all_ref = refs
    listed = listed_ref.shape[0] // nodes
    parts = all_ref.shape[0] // nodes
    used = lax.broadcasted_iota(jnp.int32, (slots, nodes), 0) < deg_ref[...]
    index = jnp.where(used, nbr_ref[...] - start * nodes, -1)
    tall = 32

    def per_rows(step, carry):
        top = pl.multiple_of(step * tall, tall)
        place = lax.broadcasted_iota(jnp.int32, (tall, nodes), 0) + top
        total = jnp.zeros((tall, nodes), F32)
        for k in range(slots):
            total = total + jnp.where(index[k : k + 1, :] == place, F32(1), F32(0))
        all_ref[pl.ds(top, tall), :] = total.astype(BF16)
        return carry

    lax.fori_loop(0, parts * nodes // tall, per_rows, jnp.int32(0))
    if before:
        listed_ref[...] = before[0][...]
    else:
        listed_ref[...] = jnp.zeros_like(listed_ref)

    def per_part(part, rank):
        fresh = is_fresh(stale_ref, start + part)
        rows = pl.ds(pl.multiple_of(part * nodes, nodes), nodes)

        @pl.when(fresh)
        def _():
            to = pl.multiple_of(jnp.minimum(rank, listed - 1) * nodes, nodes)
            listed_ref[pl.ds(to, nodes), :] = all_ref[rows, :]
            all_ref[rows, :] = jnp.zeros((nodes, nodes), BF16)

        return rank + fresh.astype(jnp.int32)

    first = sum([is_fresh(stale_ref, p).astype(jnp.int32) for p in range(start)], jnp.int32(0))
    lax.fori_loop(0, parts, per_part, first)
    share = jnp.dot(
        cache_ref[:, start * nodes : (start + parts) * nodes], all_ref[...], preferred_element_type=F32
    )
    acc_ref[...] = before[1][...] + share if before else share


def pack_body(feat_ref, self_ref, nbr_ref, cot_ref, bias_ref, out_ref, wide):
    row = 0
    for ref in (feat_ref, self_ref, nbr_ref, cot_ref):
        out_ref[row : row + ref.shape[0], :] = ref[...]
        row += ref.shape[0]
    wide[...] = jnp.zeros_like(wide)
    for i, term in enumerate(split3(bias_ref[...])):
        wide[i : i + 1, : bias_ref.shape[1]] = term
    out_ref[row:, :] = wide[...].astype(BF16)


def stack_body(*refs):
    ins, out_ref = refs[:-1], refs[-1]
    rows = ins[0].shape[0]
    for i, ref in enumerate(ins):
        out_ref[i * rows : (i + 1) * rows, :] = ref[...]


def node_weights(counts_ref, deg):
    nodes = deg.shape[1]
    live = (
        lax.broadcasted_iota(jnp.int32, (1, nodes), 1) < counts_ref[lax.axis_index("dom")]
    ).astype(F32)
    return live, live / deg.astype(F32)


def mean_body(stale_ref, counts_ref, deg_ref, acc_ref, listed_ref, *refs):
    stacks, (out_ref, total) = refs[:LOW], refs[LOW:]
    width, nodes = acc_ref.shape
    me = lax.axis_index("dom")
    total[...] = acc_ref[...]
    for low in range(LOW):
        for high in range(stacks[0].shape[0] // width):
            part = jnp.bitwise_xor(me, low + LOW * high)

            @pl.when(is_fresh(stale_ref, part))
            def _(low=low, high=high, part=part):
                row = pl.multiple_of(rank_of(stale_ref, part) * nodes, nodes)
                total[...] += jnp.dot(
                    stacks[low][high * width : (high + 1) * width, :],
                    listed_ref[pl.ds(row, nodes), :],
                    preferred_element_type=F32,
                )

    _, weight = node_weights(counts_ref, deg_ref[...])
    out_ref[...] = (total[...] * weight).astype(BF16)


def dense_body(n_col, counts_ref, deg_ref, listed_ref, feat_ref, self_ref, nbr_ref, bias_ref, cot_ref, *refs):
    aggs, packs, refs = refs[:n_col], refs[n_col : 2 * n_col - 1], refs[2 * n_col - 1 :]
    act_ref, own_ref, slots, (cot_full, bias_full, full, wide) = refs[0], refs[1], refs[2 : 2 + LOW], refs[2 + LOW :]
    width, nodes = feat_ref.shape
    part_h = cot_ref.shape[0]
    hidden = part_h * n_col
    me = lax.axis_index("col")
    live, weight = node_weights(counts_ref, deg_ref[...])
    pre = jnp.zeros((hidden, nodes), F32)
    for s in range(n_col):
        if s == 0:
            feat, w_self, w_nbr, cot, bias = feat_ref[...], self_ref[...], nbr_ref[...], cot_ref[...], bias_ref[...]
        else:
            pack = packs[s - 1]
            feat, w_self, w_nbr = [pack[i * width : (i + 1) * width, :] for i in range(3)]
            cot = pack[3 * width : 3 * width + part_h, :]
            terms = pack[3 * width + part_h :, :].astype(F32)
            bias = (terms[0:1] + terms[1:2] + terms[2:3])[:, :part_h]
        rows = pl.ds(pl.multiple_of(lax.rem(me + n_col - s, n_col) * part_h, part_h), part_h)
        cot_full[rows, :] = cot.astype(F32)
        bias_full[rows, :] = jnp.broadcast_to(bias, (LANES, part_h)).T
        for w, x in ((w_self, feat), (w_nbr, aggs[s][...])):
            pre += jnp.dot(w.astype(F32).T.astype(BF16), x, preferred_element_type=F32)
    pre += jnp.concatenate([bias_full[...]] * (nodes // LANES), 1)
    sig = 1.0 / (1.0 + jnp.exp(-pre))
    full[...] = live * pre * sig
    own_rows = pl.ds(pl.multiple_of(me * part_h, part_h), part_h)
    act_ref[...] = full[own_rows, :].astype(BF16)
    grad = (live * cot_full[...] * sig * (1.0 + pre * (1.0 - sig))).astype(BF16)
    cot_full[...] = grad.astype(F32)
    back = jnp.dot(nbr_ref[...], grad, preferred_element_type=F32)
    own_ref[...] = jnp.dot(self_ref[...], grad, preferred_element_type=F32)
    spread = (weight * back.astype(BF16).astype(F32)).astype(BF16)
    contrib = lax.dot_general(
        spread, listed_ref[...], (((1,), (1,)), ((), ())), preferred_element_type=F32
    )
    wgrads = [
        lax.dot_general(x[...], grad, (((1,), (1,)), ((), ())), preferred_element_type=F32)
        for x in (feat_ref, aggs[0])
    ]
    ones = jnp.ones((16, nodes), BF16)
    bias = lax.dot_general(
        ones, cot_full[own_rows, :].astype(BF16), (((1,), (1,)), ((), ())), preferred_element_type=F32
    )[:1]
    high = bias.astype(BF16).astype(F32)
    group = listed_ref.shape[0] // nodes // LOW
    half = width // 2
    base = group * width + half
    for q in range(LOW):
        for g in range(group):
            r = q * group + g
            wide[q, g * width : (g + 1) * width, :] = contrib[:, r * nodes : (r + 1) * nodes]
        wide[q, base - half : base, :] = wgrads[q // 2][q % 2 * half : (q % 2 + 1) * half, :]
        wide[q, base:, :] = jnp.zeros((wide.shape[1] - base, nodes), F32)
        wide[q, base : base + 1, :part_h] = high
        wide[q, base + 1 : base + 2, :part_h] = bias - high
    low = lax.axis_index("dom") % LOW
    for m in range(LOW):
        slots[m][...] = wide[jnp.bitwise_xor(low, m)].astype(BF16)


def group_sum_body(base, *refs):
    got, (out_ref, wide, full) = refs[:LOW], refs[LOW:]
    low = lax.axis_index("dom") % LOW
    for m in range(LOW):
        wide[jnp.bitwise_xor(low, m)] = got[m][...].astype(F32)
    total = wide[0] + wide[1] + wide[2] + wide[3]
    full[...] = total
    bias = total[base : base + 1] + total[base + 1 : base + 2]
    high = bias.astype(BF16).astype(F32)
    full[base : base + 1, :] = high
    full[base + 1 : base + 2, :] = bias - high
    out_ref[...] = full[...].astype(BF16)


def line_sum_body(base, width, count, stale_ref, *refs):
    got, bias_ref, outs, (wide, full, piece) = refs[:count], refs[count], refs[count + 1 : count + 1 + LOW], refs[count + 1 + LOW :]
    me = lax.axis_index("dom")
    place = me // LOW
    for m in range(count):
        wide[jnp.bitwise_xor(place, m)] = got[m][...].astype(F32)
    total = wide[0]
    for m in range(1, count):
        total += wide[m]
    full[...] = total
    bias_ref[...] = (total[base : base + 1] + total[base + 1 : base + 2])[:, : bias_ref.shape[1]]
    half = width // 2
    group = (base - half) // width
    piece[...] = jnp.zeros_like(piece)
    piece[width : width + half, :] = full[base - half : base, :]
    for m in range(LOW):
        rank = rank_of(stale_ref, jnp.bitwise_xor(me, m))
        row = pl.multiple_of(lax.rem(rank, group) * width, 8)
        piece[:width, :] = full[pl.ds(row, width), :]
        outs[m][...] = piece[...].astype(BF16)


def last_body(group, stale_ref, own_ref, *refs):
    got, (feat_ref, self_ref, nbr_ref, wide) = refs[:LOW], refs[LOW:]
    width = own_ref.shape[0]
    me = lax.axis_index("dom")
    low = me % LOW
    for m in range(LOW):
        wide[jnp.bitwise_xor(low, m)] = got[m][...].astype(F32)
    fresh = is_fresh(stale_ref, me).astype(F32)
    back = wide[rank_of(stale_ref, me) // group][:width]
    feat_ref[...] = (own_ref[...] + fresh * back).astype(BF16)
    half = width // 2
    for q in range(LOW):
        ref = nbr_ref if q // 2 else self_ref
        ref[q % 2 * half : (q % 2 + 1) * half, :] = wide[q, width : width + half, :]


def per_device(
    n_col,
    features,
    cached_embed,
    staleness,
    node_counts,
    neighbours,
    degrees,
    w_self,
    w_nbr,
    sage_bias,
    cotangent,
):
    width, nodes = features.shape
    hidden = w_self.shape[1]
    dom = staleness.shape[0]
    listed = dom // 4
    part_h = cotangent.shape[0]
    shape = jax.ShapeDtypeStruct

    def hop(block, m):
        return lax.ppermute(block, "dom", [(i, i ^ m) for i in range(dom)])

    def along(block):
        return [block] + [hop(block, m) for m in range(LOW, dom, LOW)]

    def within(slots):
        return [slots[0]] + [hop(slots[m], m) for m in range(1, LOW)]

    def around(block):
        return [
            lax.ppermute(block, "col", [(i, (i + s) % n_col) for i in range(n_col)])
            for s in range(1, n_col)
        ]

    line = along(features)
    bias_row = sage_bias.reshape(1, part_h)
    packed = call(
        pack_body,
        shape((3 * width + part_h + 16, nodes), BF16),
        0,
        5,
        [pltpu.VMEM((16, nodes), F32)],
        moved=4 * (3 * width + part_h) * nodes,
    )(features, w_self, w_nbr, cotangent, bias_row)
    packs = around(packed)
    deg = degrees.reshape(1, nodes)
    half_parts = dom // 2

    def count(start, *before):
        return call(
            functools.partial(count_body, start, dom),
            (shape((listed * nodes, nodes), BF16), shape((width, nodes), F32)),
            1,
            3 + len(before),
            [pltpu.VMEM((half_parts * nodes, nodes), BF16)],
            flops=2 * width * half_parts * nodes * nodes,
            moved=half_parts * nodes * nodes * 16,
        )(staleness, neighbours, deg, cached_embed, *before)

    before = count(0)
    stacked = call(stack_body, shape((width * len(line), nodes), BF16), 0, len(line), moved=4 * dom * width * nodes // LOW)(
        *line
    )
    stacks = within([stacked] * LOW)
    counts, acc = count(half_parts, *before)
    agg = call(
        mean_body,
        shape((width, nodes), BF16),
        2,
        3 + LOW,
        [pltpu.VMEM((width, nodes), F32)],
        moved=2 * dom * width * nodes,
    )(staleness, node_counts, deg, acc, counts, *stacks)
    aggs = [agg] + around(agg)
    group = listed // LOW
    base = group * width + width // 2
    rows = up16(base + 2)
    act, own, *slots = call(
        functools.partial(dense_body, n_col),
        [shape((part_h, nodes), BF16), shape((width, nodes), F32)] + [shape((rows, nodes), BF16)] * LOW,
        1,
        7 + 2 * n_col - 1,
        [
            pltpu.VMEM((hidden, nodes), F32),
            pltpu.VMEM((hidden, LANES), F32),
            pltpu.VMEM((hidden, nodes), F32),
            pltpu.VMEM((LOW, rows, nodes), F32),
        ],
        flops=2 * width * nodes * (hidden * 6 + listed * nodes),
        moved=4 * LOW * rows * nodes,
    )(node_counts, deg, counts, features, w_self, w_nbr, bias_row, cotangent, *aggs, *packs)
    summed = call(
        functools.partial(group_sum_body, base),
        shape((rows, nodes), BF16),
        0,
        LOW,
        [pltpu.VMEM((LOW, rows, nodes), F32), pltpu.VMEM((rows, nodes), F32)],
        moved=2 * LOW * rows * nodes,
    )(*within(slots))
    lines = along(summed)
    tall = up16(width + width // 2)
    bias, *pieces = call(
        functools.partial(line_sum_body, base, width, len(lines)),
        [shape((1, part_h), F32)] + [shape((tall, nodes), BF16)] * LOW,
        1,
        len(lines),
        [
            pltpu.VMEM((len(lines), rows, nodes), F32),
            pltpu.VMEM((rows, nodes), F32),
            pltpu.VMEM((tall, nodes), F32),
        ],
        moved=2 * len(lines) * rows * nodes,
    )(staleness, *lines)
    grad_feat, grad_self, grad_nbr = call(
        functools.partial(last_body, group),
        (shape((width, nodes), BF16), shape((width, hidden), F32), shape((width, hidden), F32)),
        1,
        1 + LOW,
        [pltpu.VMEM((LOW, tall, nodes), F32)],
        moved=2 * LOW * tall * nodes,
    )(staleness, own, *within(pieces))
    return act, grad_feat, grad_self, grad_nbr, bias.reshape(-1)


def solution(mesh):
    placed = (
        P("col", "dom"),
        P("col", None),
        P(),
        P(),
        P(None, "dom"),
        P("dom"),
        P("col", None),
        P("col", None),
        P("col"),
        P("col", "dom"),
    )
    return jax.shard_map(
        functools.partial(per_device, mesh.shape["col"]),
        mesh=mesh,
        in_specs=placed,
        out_specs=(P("col", "dom"), P("col", "dom"), P("col", None), P("col", None), P("col")),
        check_vma=False,
    )
```

```python
import functools

import jax
import jax.numpy as jnp
from jax import lax
from jax.experimental import pallas as pl
from jax.experimental.pallas import tpu as pltpu
from jax.sharding import PartitionSpec as P

LIMIT = 8
LANES = 128
LOW = 4
BF16 = jnp.bfloat16
F32 = jnp.float32
SMEM = pl.BlockSpec(memory_space=pltpu.SMEM)
VMEM = pl.BlockSpec(memory_space=pltpu.VMEM)
PARAMS = pltpu.CompilerParams(vmem_limit_bytes=32 * 1024 * 1024)


def call(body, outs, smem_count, vmem_count, scratch=(), flops=0, moved=0):
    return pl.pallas_call(
        body,
        out_shape=outs,
        in_specs=[SMEM] * smem_count + [VMEM] * vmem_count,
        out_specs=jax.tree.map(lambda _: VMEM, outs),
        scratch_shapes=list(scratch),
        compiler_params=PARAMS,
        cost_estimate=pl.CostEstimate(flops=flops, bytes_accessed=moved, transcendentals=0),
    )


def up16(rows):
    return -(-rows // 16) * 16


def is_fresh(stale_ref, part):
    return stale_ref[part] >= LIMIT


def fill_ranks(stale_ref, ranks):
    rank = jnp.int32(0)
    for p in range(stale_ref.shape[0]):
        ranks[p] = jnp.minimum(rank, stale_ref.shape[0] // 4 - 1)
        rank += is_fresh(stale_ref, p).astype(jnp.int32)


def split3(x):
    high = x.astype(BF16).astype(F32)
    mid = (x - high).astype(BF16).astype(F32)
    return high, mid, x - high - mid


def count_body(start, stale_ref, *refs):
    if start:
        nbr_ref, deg_ref, cache_ref, before, share, listed_ref, acc_ref, all_ref = refs
    else:
        counts_ref, nbr_ref, deg_ref, cache_ref, listed_ref, acc_ref, scale_ref, all_ref = refs
    slots, nodes = nbr_ref.shape
    listed = listed_ref.shape[0] // nodes
    parts = all_ref.shape[0] // nodes
    used = lax.broadcasted_iota(jnp.int32, (slots, nodes), 0) < deg_ref[...]
    index = jnp.where(used, nbr_ref[...], -1)
    tall = 16
    if start:
        listed_ref[...] = before[...]
    else:
        listed_ref[...] = jnp.zeros_like(listed_ref)
        live = (
            lax.broadcasted_iota(jnp.int32, (1, nodes), 1) < counts_ref[lax.axis_index("dom")]
        ).astype(F32)
        scale_ref[0:8, :] = jnp.broadcast_to(live, (8, nodes))
        scale_ref[8:16, :] = jnp.broadcast_to(live / deg_ref[...].astype(F32), (8, nodes))

    def per_part(part, rank):
        fresh = is_fresh(stale_ref, start + part)
        local = index - (start + part) * nodes
        local = jnp.where((local >= 0) & (local < nodes), local, -1).astype(F32)
        rows = [jnp.broadcast_to(local[k : k + 1, :], (tall, nodes)).astype(BF16) for k in range(slots)]
        for top in range(0, nodes, tall):
            place = (lax.broadcasted_iota(jnp.int32, (tall, nodes), 0) + top).astype(F32).astype(BF16)
            total = jnp.zeros((tall, nodes), BF16)
            for k in range(slots):
                total = total + jnp.where(rows[k] == place, BF16(1), BF16(0))
            all_ref[pl.ds(pl.multiple_of(part * nodes + top, tall), tall), :] = total
        block = pl.ds(pl.multiple_of(part * nodes, nodes), nodes)

        @pl.when(fresh)
        def _():
            to = pl.multiple_of(jnp.minimum(rank, listed - 1) * nodes, nodes)
            listed_ref[pl.ds(to, nodes), :] = all_ref[block, :]
            all_ref[block, :] = jnp.zeros((nodes, nodes), BF16)

        return rank + fresh.astype(jnp.int32)

    first = sum([is_fresh(stale_ref, p).astype(jnp.int32) for p in range(start)], jnp.int32(0))
    lax.fori_loop(0, parts, per_part, first)
    own = jnp.dot(
        cache_ref[:, start * nodes : (start + parts) * nodes], all_ref[...], preferred_element_type=F32
    )
    acc_ref[...] = share[...] + own if start else own


def pack_body(feat_ref, self_ref, nbr_ref, cot_ref, bias_ref, out_ref, bias, wide, sems):
    row = 0
    copies = []
    for i, ref in enumerate((feat_ref, self_ref, nbr_ref, cot_ref)):
        copies.append(pltpu.make_async_copy(ref, out_ref.at[row : row + ref.shape[0], :], sems.at[i]))
        row += ref.shape[0]
    copies.append(pltpu.make_async_copy(bias_ref, bias, sems.at[4]))
    for copy in copies:
        copy.start()
    wide[...] = jnp.zeros_like(wide)
    copies[4].wait()
    for i, term in enumerate(split3(bias[...])):
        wide[i : i + 1, : bias.shape[1]] = term
    out_ref[row:, :] = wide[...].astype(BF16)
    for copy in copies[:4]:
        copy.wait()


def stack_body(*refs):
    ins, out_ref = refs[:-1], refs[-1]
    rows = ins[0].shape[0]
    for i, ref in enumerate(ins):
        out_ref[i * rows : (i + 1) * rows, :] = ref[...]


def mean_body(stale_ref, scale_ref, acc_ref, listed_ref, *refs):
    stacks, (out_ref, blocks, ranks) = refs[:LOW], refs[LOW:]
    width, nodes = acc_ref.shape
    me = lax.axis_index("dom")
    fill_ranks(stale_ref, ranks)
    for low in range(LOW):
        for high in range(stacks[0].shape[0] // width):
            part = jnp.bitwise_xor(me, low + LOW * high)

            @pl.when(is_fresh(stale_ref, part))
            def _(low=low, high=high, part=part):
                blocks[ranks[part]] = stacks[low][high * width : (high + 1) * width, :]

    total = acc_ref[...]
    for r in range(blocks.shape[0]):
        total += jnp.dot(
            blocks[r], listed_ref[r * nodes : (r + 1) * nodes, :], preferred_element_type=F32
        )
    out_ref[...] = (total * scale_ref[8:9, :]).astype(BF16)


def dense_body(n_col, scale_ref, listed_ref, feat_ref, self_ref, nbr_ref, bias_ref, cot_ref, *refs):
    aggs, packs, refs = refs[:n_col], refs[n_col : 2 * n_col - 1], refs[2 * n_col - 1 :]
    act_ref, own_ref, slots, (cot_full, bias_full, full, wide) = refs[0], refs[1], refs[2 : 2 + LOW], refs[2 + LOW :]
    width, nodes = feat_ref.shape
    part_h = cot_ref.shape[0]
    hidden = part_h * n_col
    me = lax.axis_index("col")
    live, weight = scale_ref[0:1, :], scale_ref[8:9, :]
    pre = jnp.zeros((hidden, nodes), F32)
    for s in range(n_col):
        if s == 0:
            feat, w_self, w_nbr, cot, bias = feat_ref[...], self_ref[...], nbr_ref[...], cot_ref[...], bias_ref[...]
        else:
            pack = packs[s - 1]
            feat, w_self, w_nbr = [pack[i * width : (i + 1) * width, :] for i in range(3)]
            cot = pack[3 * width : 3 * width + part_h, :]
            terms = pack[3 * width + part_h :, :].astype(F32)
            bias = (terms[0:1] + terms[1:2] + terms[2:3])[:, :part_h]
        rows = pl.ds(pl.multiple_of(lax.rem(me + n_col - s, n_col) * part_h, part_h), part_h)
        cot_full[rows, :] = cot.astype(F32)
        bias_full[rows, :] = jnp.broadcast_to(bias, (LANES, part_h)).T
        for w, x in ((w_self, feat), (w_nbr, aggs[s][...])):
            pre += jnp.dot(w.astype(F32).T.astype(BF16), x, preferred_element_type=F32)
    pre += jnp.concatenate([bias_full[...]] * (nodes // LANES), 1)
    sig = 1.0 / (1.0 + jnp.exp(-pre))
    full[...] = live * pre * sig
    own_rows = pl.ds(pl.multiple_of(me * part_h, part_h), part_h)
    act_ref[...] = full[own_rows, :].astype(BF16)
    grad = (live * cot_full[...] * sig * (1.0 + pre * (1.0 - sig))).astype(BF16)
    cot_full[...] = grad.astype(F32)
    back = jnp.dot(nbr_ref[...], grad, preferred_element_type=F32)
    own_ref[...] = jnp.dot(self_ref[...], grad, preferred_element_type=F32)
    spread = (weight * back.astype(BF16).astype(F32)).astype(BF16)
    contrib = lax.dot_general(
        spread, listed_ref[...], (((1,), (1,)), ((), ())), preferred_element_type=F32
    )
    wgrads = [
        lax.dot_general(x[...], grad, (((1,), (1,)), ((), ())), preferred_element_type=F32)
        for x in (feat_ref, aggs[0])
    ]
    ones = jnp.ones((16, nodes), BF16)
    bias = lax.dot_general(
        ones, cot_full[own_rows, :].astype(BF16), (((1,), (1,)), ((), ())), preferred_element_type=F32
    )[:1]
    high = bias.astype(BF16).astype(F32)
    listed = listed_ref.shape[0] // nodes
    half, short = width // 2, width // LOW
    base = listed * short + half
    for q in range(LOW):
        for r in range(listed):
            wide[q, r * short : (r + 1) * short, :] = contrib[
                q * short : (q + 1) * short, r * nodes : (r + 1) * nodes
            ]
        wide[q, base - half : base, :] = wgrads[q // 2][q % 2 * half : (q % 2 + 1) * half, :]
        wide[q, base:, :] = jnp.zeros((wide.shape[1] - base, nodes), F32)
        wide[q, base : base + 1, :part_h] = high
        wide[q, base + 1 : base + 2, :part_h] = bias - high
    low = lax.axis_index("dom") % LOW
    for m in range(LOW):
        slots[m][...] = wide[jnp.bitwise_xor(low, m)].astype(BF16)


def group_sum_body(base, *refs):
    got, (out_ref, wide, full) = refs[:LOW], refs[LOW:]
    low = lax.axis_index("dom") % LOW
    for m in range(LOW):
        wide[jnp.bitwise_xor(low, m)] = got[m][...].astype(F32)
    total = wide[0] + wide[1] + wide[2] + wide[3]
    full[...] = total
    bias = total[base : base + 1] + total[base + 1 : base + 2]
    high = bias.astype(BF16).astype(F32)
    full[base : base + 1, :] = high
    full[base + 1 : base + 2, :] = bias - high
    out_ref[...] = full[...].astype(BF16)


def line_sum_body(base, width, count, stale_ref, *refs):
    got, bias_ref, outs = refs[:count], refs[count], refs[count + 1 : count + 1 + LOW]
    wide, kept, piece, ranks = refs[count + 1 + LOW :]
    me = lax.axis_index("dom")
    place = me // LOW
    for m in range(count):
        wide[jnp.bitwise_xor(place, m)] = got[m][...].astype(F32)
    total = wide[0]
    for m in range(1, count):
        total += wide[m]
    bias_ref[...] = (total[base : base + 1] + total[base + 1 : base + 2])[:, : bias_ref.shape[1]]
    half, short = width // 2, width // LOW
    for r in range(kept.shape[0]):
        kept[r] = total[r * short : (r + 1) * short]
    piece[...] = jnp.zeros_like(piece)
    piece[short : short + half, :] = total[base - half : base]
    fill_ranks(stale_ref, ranks)
    for m in range(LOW):
        piece[:short, :] = kept[ranks[jnp.bitwise_xor(me, m)]]
        outs[m][...] = piece[...].astype(BF16)


def last_body(stale_ref, own_ref, *refs):
    got, (feat_ref, self_ref, nbr_ref, wide, back) = refs[:LOW], refs[LOW:]
    width = own_ref.shape[0]
    me = lax.axis_index("dom")
    low = me % LOW
    half, short = width // 2, width // LOW
    for m in range(LOW):
        wide[jnp.bitwise_xor(low, m)] = got[m][...].astype(F32)
    fresh = is_fresh(stale_ref, me).astype(F32)
    for q in range(LOW):
        back[q * short : (q + 1) * short, :] = wide[q, :short]
        ref = nbr_ref if q // 2 else self_ref
        ref[q % 2 * half : (q % 2 + 1) * half, :] = wide[q, short : short + half]
    feat_ref[...] = (own_ref[...] + fresh * back[...]).astype(BF16)


def per_device(
    n_col,
    features,
    cached_embed,
    staleness,
    node_counts,
    neighbours,
    degrees,
    w_self,
    w_nbr,
    sage_bias,
    cotangent,
):
    width, nodes = features.shape
    hidden = w_self.shape[1]
    dom = staleness.shape[0]
    listed = dom // 4
    part_h = cotangent.shape[0]
    shape = jax.ShapeDtypeStruct

    def hop(block, m):
        return lax.ppermute(block, "dom", [(i, i ^ m) for i in range(dom)])

    def along(block):
        return [block] + [hop(block, m) for m in range(LOW, dom, LOW)]

    def within(slots):
        return [slots[0]] + [hop(slots[m], m) for m in range(1, LOW)]

    def around(block):
        return [
            lax.ppermute(block, "col", [(i, (i + s) % n_col) for i in range(n_col)])
            for s in range(1, n_col)
        ]

    line = along(features)
    bias_row = sage_bias.reshape(1, part_h)
    packed = pl.pallas_call(
        pack_body,
        out_shape=shape((3 * width + part_h + 16, nodes), BF16),
        in_specs=[pl.BlockSpec(memory_space=pltpu.HBM)] * 5,
        out_specs=VMEM,
        scratch_shapes=[
            pltpu.VMEM((1, part_h), F32),
            pltpu.VMEM((16, nodes), F32),
            pltpu.SemaphoreType.DMA((5,)),
        ],
        compiler_params=PARAMS,
        cost_estimate=pl.CostEstimate(
            flops=0, bytes_accessed=4 * (3 * width + part_h) * nodes, transcendentals=0
        ),
    )(features, w_self, w_nbr, cotangent, bias_row)
    packs = around(packed)
    deg = degrees.reshape(1, nodes)
    half_parts = dom // 2

    sums = (shape((listed * nodes, nodes), BF16), shape((width, nodes), F32))
    counting = dict(
        scratch=[pltpu.VMEM((half_parts * nodes, nodes), BF16)],
        flops=2 * width * half_parts * nodes * nodes,
        moved=half_parts * nodes * nodes * 16,
    )
    before, share, scale = call(
        functools.partial(count_body, 0), sums + (shape((16, nodes), F32),), 2, 3, **counting
    )(staleness, node_counts, neighbours, deg, cached_embed)
    *others, before = lax.optimization_barrier((*line[1:], before))
    line = line[:1] + others
    stacked = call(stack_body, shape((width * len(line), nodes), BF16), 0, len(line), moved=4 * dom * width * nodes // LOW)(
        *line
    )
    stacks = within([stacked] * LOW)
    counts, acc = call(functools.partial(count_body, half_parts), sums, 1, 5, **counting)(
        staleness, neighbours, deg, cached_embed, before, share
    )
    agg = call(
        mean_body,
        shape((width, nodes), BF16),
        1,
        3 + LOW,
        [pltpu.VMEM((listed, width, nodes), BF16), pltpu.SMEM((dom,), jnp.int32)],
        moved=2 * dom * width * nodes,
    )(staleness, scale, acc, counts, *stacks)
    aggs = [agg] + around(agg)
    base = listed * (width // LOW) + width // 2
    rows = up16(base + 2)
    act, own, *slots = call(
        functools.partial(dense_body, n_col),
        [shape((part_h, nodes), BF16), shape((width, nodes), F32)] + [shape((rows, nodes), BF16)] * LOW,
        0,
        7 + 2 * n_col - 1,
        [
            pltpu.VMEM((hidden, nodes), F32),
            pltpu.VMEM((hidden, LANES), F32),
            pltpu.VMEM((hidden, nodes), F32),
            pltpu.VMEM((LOW, rows, nodes), F32),
        ],
        flops=2 * width * nodes * (hidden * 6 + listed * nodes),
        moved=4 * LOW * rows * nodes,
    )(scale, counts, features, w_self, w_nbr, bias_row, cotangent, *aggs, *packs)
    summed = call(
        functools.partial(group_sum_body, base),
        shape((rows, nodes), BF16),
        0,
        LOW,
        [pltpu.VMEM((LOW, rows, nodes), F32), pltpu.VMEM((rows, nodes), F32)],
        moved=2 * LOW * rows * nodes,
    )(*within(slots))
    lines = along(summed)
    tall = up16(width // LOW + width // 2)
    bias, *pieces = call(
        functools.partial(line_sum_body, base, width, len(lines)),
        [shape((1, part_h), F32)] + [shape((tall, nodes), BF16)] * LOW,
        1,
        len(lines),
        [
            pltpu.VMEM((len(lines), rows, nodes), F32),
            pltpu.VMEM((listed, width // LOW, nodes), F32),
            pltpu.VMEM((tall, nodes), F32),
            pltpu.SMEM((dom,), jnp.int32),
        ],
        moved=2 * len(lines) * rows * nodes,
    )(staleness, *lines)
    grad_feat, grad_self, grad_nbr = call(
        last_body,
        (shape((width, nodes), BF16), shape((width, hidden), F32), shape((width, hidden), F32)),
        1,
        1 + LOW,
        [pltpu.VMEM((LOW, tall, nodes), F32), pltpu.VMEM((width, nodes), F32)],
        moved=2 * LOW * tall * nodes,
    )(staleness, own, *within(pieces))
    return act, grad_feat, grad_self, grad_nbr, bias.reshape(-1)


def solution(mesh):
    placed = (
        P("col", "dom"),
        P("col", None),
        P(),
        P(),
        P(None, "dom"),
        P("dom"),
        P("col", None),
        P("col", None),
        P("col"),
        P("col", "dom"),
    )
    return jax.shard_map(
        functools.partial(per_device, mesh.shape["col"]),
        mesh=mesh,
        in_specs=placed,
        out_specs=(P("col", "dom"), P("col", "dom"), P("col", None), P("col", None), P("col")),
        check_vma=False,
    )
```

```python
import functools

import jax
import jax.numpy as jnp
from jax import lax
from jax.experimental import pallas as pl
from jax.experimental.pallas import tpu as pltpu
from jax.sharding import PartitionSpec as P

LIMIT = 8
LANES = 128
LOW = 4
BF16 = jnp.bfloat16
F32 = jnp.float32
SMEM = pl.BlockSpec(memory_space=pltpu.SMEM)
VMEM = pl.BlockSpec(memory_space=pltpu.VMEM)
HBM = pl.BlockSpec(memory_space=pltpu.HBM)
PARAMS = pltpu.CompilerParams(vmem_limit_bytes=32 * 1024 * 1024)
WHOLE = pltpu.CompilerParams(vmem_limit_bytes=60 * 1024 * 1024)


def call(body, outs, smem_count, vmem_count, scratch=(), flops=0, moved=0, hbm_count=0):
    return pl.pallas_call(
        body,
        out_shape=outs,
        in_specs=[SMEM] * smem_count + [HBM] * hbm_count + [VMEM] * vmem_count,
        out_specs=jax.tree.map(lambda _: VMEM, outs),
        scratch_shapes=list(scratch),
        compiler_params=WHOLE if hbm_count else PARAMS,
        cost_estimate=pl.CostEstimate(flops=flops, bytes_accessed=moved, transcendentals=0),
    )


def up16(rows):
    return -(-rows // 16) * 16


def is_fresh(stale_ref, part):
    return stale_ref[part] >= LIMIT


def fill_ranks(stale_ref, ranks):
    rank = jnp.int32(0)
    for p in range(stale_ref.shape[0]):
        ranks[p] = jnp.minimum(rank, stale_ref.shape[0] // 4 - 1)
        rank += is_fresh(stale_ref, p).astype(jnp.int32)


def split3(x):
    high = x.astype(BF16).astype(F32)
    mid = (x - high).astype(BF16).astype(F32)
    return high, mid, x - high - mid


def count_body(stale_ref, counts_ref, nbr_ref, deg_ref, cache_ref, listed_ref, acc_ref, scale_ref, all_ref):
    slots, nodes = nbr_ref.shape
    listed = listed_ref.shape[0] // nodes
    used = lax.broadcasted_iota(jnp.int32, (slots, nodes), 0) < deg_ref[...]
    index = jnp.where(used, nbr_ref[...], -1)
    tall = 16
    live = (
        lax.broadcasted_iota(jnp.int32, (1, nodes), 1) < counts_ref[lax.axis_index("dom")]
    ).astype(F32)
    scale_ref[0:8, :] = jnp.broadcast_to(live, (8, nodes))
    scale_ref[8:16, :] = jnp.broadcast_to(live / deg_ref[...].astype(F32), (8, nodes))

    def per_part(part, rank):
        fresh = is_fresh(stale_ref, part)
        local = index - part * nodes
        local = jnp.where((local >= 0) & (local < nodes), local, -1).astype(F32)
        rows = [jnp.broadcast_to(local[k : k + 1, :], (tall, nodes)).astype(BF16) for k in range(slots)]
        for top in range(0, nodes, tall):
            place = (lax.broadcasted_iota(jnp.int32, (tall, nodes), 0) + top).astype(F32).astype(BF16)
            total = jnp.zeros((tall, nodes), BF16)
            for k in range(slots):
                total = total + jnp.where(rows[k] == place, BF16(1), BF16(0))
            all_ref[pl.ds(pl.multiple_of(part * nodes + top, tall), tall), :] = total
        block = pl.ds(pl.multiple_of(part * nodes, nodes), nodes)

        @pl.when(fresh)
        def _():
            to = pl.multiple_of(jnp.minimum(rank, listed - 1) * nodes, nodes)
            listed_ref[pl.ds(to, nodes), :] = all_ref[block, :]
            all_ref[block, :] = jnp.zeros((nodes, nodes), BF16)

        return rank + fresh.astype(jnp.int32)

    lax.fori_loop(0, stale_ref.shape[0], per_part, jnp.int32(0))
    acc_ref[...] = jnp.dot(cache_ref[...], all_ref[...], preferred_element_type=F32)


def pack_body(feat_ref, self_ref, nbr_ref, cot_ref, bias_ref, out_ref, bias, wide, sems):
    row = 0
    copies = []
    for i, ref in enumerate((feat_ref, self_ref, nbr_ref, cot_ref)):
        copies.append(pltpu.make_async_copy(ref, out_ref.at[row : row + ref.shape[0], :], sems.at[i]))
        row += ref.shape[0]
    copies.append(pltpu.make_async_copy(bias_ref, bias, sems.at[4]))
    for copy in copies:
        copy.start()
    wide[...] = jnp.zeros_like(wide)
    copies[4].wait()
    for i, term in enumerate(split3(bias[...])):
        wide[i : i + 1, : bias.shape[1]] = term
    out_ref[row:, :] = wide[...].astype(BF16)
    for copy in copies[:4]:
        copy.wait()


def stack_body(*refs):
    ins, out_ref = refs[:-1], refs[-1]
    rows = ins[0].shape[0]
    for i, ref in enumerate(ins):
        out_ref[i * rows : (i + 1) * rows, :] = ref[...]


def mean_body(stale_ref, scale_ref, acc_ref, listed_ref, *refs):
    stacks, (out_ref, blocks, ranks) = refs[:LOW], refs[LOW:]
    width, nodes = acc_ref.shape
    me = lax.axis_index("dom")
    fill_ranks(stale_ref, ranks)
    for low in range(LOW):
        for high in range(stacks[0].shape[0] // width):
            part = jnp.bitwise_xor(me, low + LOW * high)

            @pl.when(is_fresh(stale_ref, part))
            def _(low=low, high=high, part=part):
                blocks[ranks[part]] = stacks[low][high * width : (high + 1) * width, :]

    total = acc_ref[...]
    for r in range(blocks.shape[0]):
        total += jnp.dot(
            blocks[r], listed_ref[r * nodes : (r + 1) * nodes, :], preferred_element_type=F32
        )
    out_ref[...] = (total * scale_ref[8:9, :]).astype(BF16)


def dense_body(n_col, scale_ref, listed_ref, feat_ref, self_ref, nbr_ref, bias_ref, cot_ref, *refs):
    aggs, packs, refs = refs[:n_col], refs[n_col : 2 * n_col - 1], refs[2 * n_col - 1 :]
    act_ref, own_ref, slots, (cot_full, bias_full, full, wide) = refs[0], refs[1], refs[2 : 2 + LOW], refs[2 + LOW :]
    width, nodes = feat_ref.shape
    part_h = cot_ref.shape[0]
    hidden = part_h * n_col
    me = lax.axis_index("col")
    live, weight = scale_ref[0:1, :], scale_ref[8:9, :]
    pre = jnp.zeros((hidden, nodes), F32)
    for s in range(n_col):
        if s == 0:
            feat, w_self, w_nbr, cot, bias = feat_ref[...], self_ref[...], nbr_ref[...], cot_ref[...], bias_ref[...]
        else:
            pack = packs[s - 1]
            feat, w_self, w_nbr = [pack[i * width : (i + 1) * width, :] for i in range(3)]
            cot = pack[3 * width : 3 * width + part_h, :]
            terms = pack[3 * width + part_h :, :].astype(F32)
            bias = (terms[0:1] + terms[1:2] + terms[2:3])[:, :part_h]
        rows = pl.ds(pl.multiple_of(lax.rem(me + n_col - s, n_col) * part_h, part_h), part_h)
        cot_full[rows, :] = cot.astype(F32)
        bias_full[rows, :] = jnp.broadcast_to(bias, (LANES, part_h)).T
        for w, x in ((w_self, feat), (w_nbr, aggs[s][...])):
            pre += jnp.dot(w.astype(F32).T.astype(BF16), x, preferred_element_type=F32)
    pre += jnp.concatenate([bias_full[...]] * (nodes // LANES), 1)
    sig = 1.0 / (1.0 + jnp.exp(-pre))
    full[...] = live * pre * sig
    own_rows = pl.ds(pl.multiple_of(me * part_h, part_h), part_h)
    act_ref[...] = full[own_rows, :].astype(BF16)
    grad = (live * cot_full[...] * sig * (1.0 + pre * (1.0 - sig))).astype(BF16)
    cot_full[...] = grad.astype(F32)
    back = jnp.dot(nbr_ref[...], grad, preferred_element_type=F32)
    own_ref[...] = jnp.dot(self_ref[...], grad, preferred_element_type=F32)
    spread = (weight * back.astype(BF16).astype(F32)).astype(BF16)
    contrib = lax.dot_general(
        spread, listed_ref[...], (((1,), (1,)), ((), ())), preferred_element_type=F32
    )
    wgrads = [
        lax.dot_general(x[...], grad, (((1,), (1,)), ((), ())), preferred_element_type=F32)
        for x in (feat_ref, aggs[0])
    ]
    ones = jnp.ones((16, nodes), BF16)
    bias = lax.dot_general(
        ones, cot_full[own_rows, :].astype(BF16), (((1,), (1,)), ((), ())), preferred_element_type=F32
    )[:1]
    high = bias.astype(BF16).astype(F32)
    listed = listed_ref.shape[0] // nodes
    half, short = width // 2, width // LOW
    base = listed * short + half
    for q in range(LOW):
        for r in range(listed):
            wide[q, r * short : (r + 1) * short, :] = contrib[
                q * short : (q + 1) * short, r * nodes : (r + 1) * nodes
            ]
        wide[q, base - half : base, :] = wgrads[q // 2][q % 2 * half : (q % 2 + 1) * half, :]
        wide[q, base:, :] = jnp.zeros((wide.shape[1] - base, nodes), F32)
        wide[q, base : base + 1, :part_h] = high
        wide[q, base + 1 : base + 2, :part_h] = bias - high
    low = lax.axis_index("dom") % LOW
    for m in range(LOW):
        slots[m][...] = wide[jnp.bitwise_xor(low, m)].astype(BF16)


def group_sum_body(base, *refs):
    got, (out_ref, wide, full) = refs[:LOW], refs[LOW:]
    low = lax.axis_index("dom") % LOW
    for m in range(LOW):
        wide[jnp.bitwise_xor(low, m)] = got[m][...].astype(F32)
    total = wide[0] + wide[1] + wide[2] + wide[3]
    full[...] = total
    bias = total[base : base + 1] + total[base + 1 : base + 2]
    high = bias.astype(BF16).astype(F32)
    full[base : base + 1, :] = high
    full[base + 1 : base + 2, :] = bias - high
    out_ref[...] = full[...].astype(BF16)


def line_sum_body(base, width, count, stale_ref, *refs):
    got, bias_ref, outs = refs[:count], refs[count], refs[count + 1 : count + 1 + LOW]
    wide, kept, piece, ranks = refs[count + 1 + LOW :]
    me = lax.axis_index("dom")
    place = me // LOW
    for m in range(count):
        wide[jnp.bitwise_xor(place, m)] = got[m][...].astype(F32)
    total = wide[0]
    for m in range(1, count):
        total += wide[m]
    bias_ref[...] = jnp.broadcast_to(total[base : base + 1] + total[base + 1 : base + 2], bias_ref.shape)
    half, short = width // 2, width // LOW
    for r in range(kept.shape[0]):
        kept[r] = total[r * short : (r + 1) * short]
    piece[...] = jnp.zeros_like(piece)
    piece[short : short + half, :] = total[base - half : base]
    fill_ranks(stale_ref, ranks)
    for m in range(LOW):
        piece[:short, :] = kept[ranks[jnp.bitwise_xor(me, m)]]
        outs[m][...] = piece[...].astype(BF16)


def last_body(stale_ref, act_ref, bias_ref, own_ref, *refs):
    got, (act_out, feat_ref, self_ref, nbr_ref, bias_out, wide, back) = refs[:LOW], refs[LOW:]
    act_out[...] = act_ref[...]
    bias_out[...] = bias_ref[:1, : bias_out.shape[1]]
    width = own_ref.shape[0]
    me = lax.axis_index("dom")
    low = me % LOW
    half, short = width // 2, width // LOW
    for m in range(LOW):
        wide[jnp.bitwise_xor(low, m)] = got[m][...].astype(F32)
    fresh = is_fresh(stale_ref, me).astype(F32)
    for q in range(LOW):
        back[q * short : (q + 1) * short, :] = wide[q, :short]
        ref = nbr_ref if q // 2 else self_ref
        ref[q % 2 * half : (q % 2 + 1) * half, :] = wide[q, short : short + half]
    feat_ref[...] = (own_ref[...] + fresh * back[...]).astype(BF16)


def per_device(
    n_col,
    features,
    cached_embed,
    staleness,
    node_counts,
    neighbours,
    degrees,
    w_self,
    w_nbr,
    sage_bias,
    cotangent,
):
    width, nodes = features.shape
    hidden = w_self.shape[1]
    dom = staleness.shape[0]
    listed = dom // 4
    part_h = cotangent.shape[0]
    shape = jax.ShapeDtypeStruct

    def hop(block, m):
        return lax.ppermute(block, "dom", [(i, i ^ m) for i in range(dom)])

    def along(block):
        return [block] + [hop(block, m) for m in range(LOW, dom, LOW)]

    def within(slots):
        return [slots[0]] + [hop(slots[m], m) for m in range(1, LOW)]

    def around(block):
        return [
            lax.ppermute(block, "col", [(i, (i + s) % n_col) for i in range(n_col)])
            for s in range(1, n_col)
        ]

    line = along(features)
    bias_row = sage_bias.reshape(1, part_h)
    packed = call(
        pack_body,
        shape((3 * width + part_h + 16, nodes), BF16),
        0,
        0,
        [pltpu.VMEM((1, part_h), F32), pltpu.VMEM((16, nodes), F32), pltpu.SemaphoreType.DMA((5,))],
        moved=4 * (3 * width + part_h) * nodes,
        hbm_count=5,
    )(features, w_self, w_nbr, cotangent, bias_row)
    packs = around(packed)
    deg = degrees.reshape(1, nodes)
    stacked = call(stack_body, shape((width * len(line), nodes), BF16), 0, len(line), moved=4 * dom * width * nodes // LOW)(
        *line
    )
    stacks = within([stacked] * LOW)
    counts, acc, scale = call(
        count_body,
        (shape((listed * nodes, nodes), BF16), shape((width, nodes), F32), shape((16, nodes), F32)),
        2,
        3,
        [pltpu.VMEM((dom * nodes, nodes), BF16)],
        flops=2 * width * dom * nodes * nodes,
        moved=dom * nodes * nodes * 16,
    )(staleness, node_counts, neighbours, deg, cached_embed)
    agg = call(
        mean_body,
        shape((width, nodes), BF16),
        1,
        3 + LOW,
        [pltpu.VMEM((listed, width, nodes), BF16), pltpu.SMEM((dom,), jnp.int32)],
        moved=2 * dom * width * nodes,
    )(staleness, scale, acc, counts, *stacks)
    aggs = [agg] + around(agg)
    base = listed * (width // LOW) + width // 2
    rows = up16(base + 2)
    act, own, *slots = call(
        functools.partial(dense_body, n_col),
        [shape((part_h, nodes), BF16), shape((width, nodes), F32)] + [shape((rows, nodes), BF16)] * LOW,
        0,
        7 + 2 * n_col - 1,
        [
            pltpu.VMEM((hidden, nodes), F32),
            pltpu.VMEM((hidden, LANES), F32),
            pltpu.VMEM((hidden, nodes), F32),
            pltpu.VMEM((LOW, rows, nodes), F32),
        ],
        flops=2 * width * nodes * (hidden * 6 + listed * nodes),
        moved=4 * LOW * rows * nodes,
    )(scale, counts, features, w_self, w_nbr, bias_row, cotangent, *aggs, *packs)
    summed = call(
        functools.partial(group_sum_body, base),
        shape((rows, nodes), BF16),
        0,
        LOW,
        [pltpu.VMEM((LOW, rows, nodes), F32), pltpu.VMEM((rows, nodes), F32)],
        moved=2 * LOW * rows * nodes,
    )(*within(slots))
    lines = along(summed)
    tall = up16(width // LOW + width // 2)
    bias, *pieces = call(
        functools.partial(line_sum_body, base, width, len(lines)),
        [shape((8, nodes), F32)] + [shape((tall, nodes), BF16)] * LOW,
        1,
        len(lines),
        [
            pltpu.VMEM((len(lines), rows, nodes), F32),
            pltpu.VMEM((listed, width // LOW, nodes), F32),
            pltpu.VMEM((tall, nodes), F32),
            pltpu.SMEM((dom,), jnp.int32),
        ],
        moved=2 * len(lines) * rows * nodes,
    )(staleness, *lines)
    act, grad_feat, grad_self, grad_nbr, bias = call(
        last_body,
        (
            shape((part_h, nodes), BF16),
            shape((width, nodes), BF16),
            shape((width, hidden), F32),
            shape((width, hidden), F32),
            shape((1, part_h), F32),
        ),
        1,
        3 + LOW,
        [pltpu.VMEM((LOW, tall, nodes), F32), pltpu.VMEM((width, nodes), F32)],
        moved=2 * LOW * tall * nodes,
    )(staleness, act, bias, own, *within(pieces))
    return act, grad_feat, grad_self, grad_nbr, bias.reshape(-1)


def solution(mesh):
    placed = (
        P("col", "dom"),
        P("col", None),
        P(),
        P(),
        P(None, "dom"),
        P("dom"),
        P("col", None),
        P("col", None),
        P("col"),
        P("col", "dom"),
    )
    return jax.shard_map(
        functools.partial(per_device, mesh.shape["col"]),
        mesh=mesh,
        in_specs=placed,
        out_specs=(P("col", "dom"), P("col", "dom"), P("col", None), P("col", None), P("col")),
        check_vma=False,
    )
```

```python
import functools

import jax
import jax.numpy as jnp
from jax import lax
from jax.experimental import pallas as pl
from jax.experimental.pallas import tpu as pltpu
from jax.sharding import PartitionSpec as P

LIMIT = 8
LANES = 128
LOW = 4
BF16 = jnp.bfloat16
F32 = jnp.float32
SMEM = pl.BlockSpec(memory_space=pltpu.SMEM)
VMEM = pl.BlockSpec(memory_space=pltpu.VMEM)
HBM = pl.BlockSpec(memory_space=pltpu.HBM)
PARAMS = pltpu.CompilerParams(vmem_limit_bytes=32 * 1024 * 1024)
WHOLE = pltpu.CompilerParams(vmem_limit_bytes=60 * 1024 * 1024)


def call(body, outs, smem_count, vmem_count, scratch=(), flops=0, moved=0, hbm_count=0):
    return pl.pallas_call(
        body,
        out_shape=outs,
        in_specs=[SMEM] * smem_count + [HBM] * hbm_count + [VMEM] * vmem_count,
        out_specs=jax.tree.map(lambda _: VMEM, outs),
        scratch_shapes=list(scratch),
        compiler_params=WHOLE if hbm_count else PARAMS,
        cost_estimate=pl.CostEstimate(flops=flops, bytes_accessed=moved, transcendentals=0),
    )


def up16(rows):
    return -(-rows // 16) * 16


def is_fresh(stale_ref, part):
    return stale_ref[part] >= LIMIT


def fill_ranks(stale_ref, ranks):
    rank = jnp.int32(0)
    for p in range(stale_ref.shape[0]):
        ranks[p] = jnp.minimum(rank, stale_ref.shape[0] // 4 - 1)
        rank += is_fresh(stale_ref, p).astype(jnp.int32)


def split3(x):
    high = x.astype(BF16).astype(F32)
    mid = (x - high).astype(BF16).astype(F32)
    return high, mid, x - high - mid


def count_body(stale_ref, counts_ref, nbr_ref, deg_ref, cache_ref, listed_ref, acc_ref, scale_ref, all_ref):
    slots, nodes = nbr_ref.shape
    listed = listed_ref.shape[0] // nodes
    used = lax.broadcasted_iota(jnp.int32, (slots, nodes), 0) < deg_ref[...]
    index = jnp.where(used, nbr_ref[...], -1)
    tall = 16
    live = (
        lax.broadcasted_iota(jnp.int32, (1, nodes), 1) < counts_ref[lax.axis_index("dom")]
    ).astype(F32)
    scale_ref[0:8, :] = jnp.broadcast_to(live, (8, nodes))
    scale_ref[8:16, :] = jnp.broadcast_to(live / deg_ref[...].astype(F32), (8, nodes))

    def per_part(part, rank):
        fresh = is_fresh(stale_ref, part)
        local = index - part * nodes
        local = jnp.where((local >= 0) & (local < nodes), local, -1).astype(F32)
        rows = [jnp.broadcast_to(local[k : k + 1, :], (tall, nodes)).astype(BF16) for k in range(slots)]
        for top in range(0, nodes, tall):
            place = (lax.broadcasted_iota(jnp.int32, (tall, nodes), 0) + top).astype(F32).astype(BF16)
            total = jnp.zeros((tall, nodes), BF16)
            for k in range(slots):
                total = total + jnp.where(rows[k] == place, BF16(1), BF16(0))
            all_ref[pl.ds(pl.multiple_of(part * nodes + top, tall), tall), :] = total
        block = pl.ds(pl.multiple_of(part * nodes, nodes), nodes)

        @pl.when(fresh)
        def _():
            to = pl.multiple_of(jnp.minimum(rank, listed - 1) * nodes, nodes)
            listed_ref[pl.ds(to, nodes), :] = all_ref[block, :]
            all_ref[block, :] = jnp.zeros((nodes, nodes), BF16)

        return rank + fresh.astype(jnp.int32)

    lax.fori_loop(0, stale_ref.shape[0], per_part, jnp.int32(0))
    acc_ref[...] = jnp.dot(cache_ref[...], all_ref[...], preferred_element_type=F32)


def pack_body(feat_ref, self_ref, nbr_ref, cot_ref, bias_ref, out_ref, bias, wide, sems):
    row = 0
    copies = []
    for i, ref in enumerate((feat_ref, self_ref, nbr_ref, cot_ref)):
        copies.append(pltpu.make_async_copy(ref, out_ref.at[row : row + ref.shape[0], :], sems.at[i]))
        row += ref.shape[0]
    copies.append(pltpu.make_async_copy(bias_ref, bias, sems.at[4]))
    for copy in copies:
        copy.start()
    wide[...] = jnp.zeros_like(wide)
    copies[4].wait()
    for i, term in enumerate(split3(bias[...])):
        wide[i : i + 1, : bias.shape[1]] = term
    out_ref[row:, :] = wide[...].astype(BF16)
    for copy in copies[:4]:
        copy.wait()


def stack_body(*refs):
    ins, out_ref = refs[:-1], refs[-1]
    rows = ins[0].shape[0]
    for i, ref in enumerate(ins):
        out_ref[i * rows : (i + 1) * rows, :] = ref[...]


def mean_body(stale_ref, scale_ref, acc_ref, listed_ref, *refs):
    stacks, (out_ref, blocks, ranks) = refs[:LOW], refs[LOW:]
    width, nodes = acc_ref.shape
    me = lax.axis_index("dom")
    fill_ranks(stale_ref, ranks)
    for low in range(LOW):
        for high in range(stacks[0].shape[0] // width):
            part = jnp.bitwise_xor(me, low + LOW * high)

            @pl.when(is_fresh(stale_ref, part))
            def _(low=low, high=high, part=part):
                blocks[ranks[part]] = stacks[low][high * width : (high + 1) * width, :]

    total = acc_ref[...]
    for r in range(blocks.shape[0]):
        total += jnp.dot(
            blocks[r], listed_ref[r * nodes : (r + 1) * nodes, :], preferred_element_type=F32
        )
    out_ref[...] = (total * scale_ref[8:9, :]).astype(BF16)


def dense_body(n_col, scale_ref, listed_ref, feat_ref, self_ref, nbr_ref, bias_ref, cot_ref, *refs):
    aggs, packs, refs = refs[:n_col], refs[n_col : 2 * n_col - 1], refs[2 * n_col - 1 :]
    act_ref, own_ref, slot_ref, cot_full, bias_full, full, wide = refs
    width, nodes = feat_ref.shape
    part_h = cot_ref.shape[0]
    hidden = part_h * n_col
    me = lax.axis_index("col")
    live, weight = scale_ref[0:1, :], scale_ref[8:9, :]
    pre = jnp.zeros((hidden, nodes), F32)
    for s in range(n_col):
        if s == 0:
            feat, w_self, w_nbr, cot, bias = feat_ref[...], self_ref[...], nbr_ref[...], cot_ref[...], bias_ref[...]
        else:
            pack = packs[s - 1]
            feat, w_self, w_nbr = [pack[i * width : (i + 1) * width, :] for i in range(3)]
            cot = pack[3 * width : 3 * width + part_h, :]
            terms = pack[3 * width + part_h :, :].astype(F32)
            bias = (terms[0:1] + terms[1:2] + terms[2:3])[:, :part_h]
        rows = pl.ds(pl.multiple_of(lax.rem(me + n_col - s, n_col) * part_h, part_h), part_h)
        cot_full[rows, :] = cot.astype(F32)
        bias_full[rows, :] = jnp.broadcast_to(bias, (LANES, part_h)).T
        for w, x in ((w_self, feat), (w_nbr, aggs[s][...])):
            pre += jnp.dot(w.astype(F32).T.astype(BF16), x, preferred_element_type=F32)
    pre += jnp.concatenate([bias_full[...]] * (nodes // LANES), 1)
    sig = 1.0 / (1.0 + jnp.exp(-pre))
    full[...] = live * pre * sig
    own_rows = pl.ds(pl.multiple_of(me * part_h, part_h), part_h)
    act_ref[...] = full[own_rows, :].astype(BF16)
    grad = (live * cot_full[...] * sig * (1.0 + pre * (1.0 - sig))).astype(BF16)
    cot_full[...] = grad.astype(F32)
    back = jnp.dot(nbr_ref[...], grad, preferred_element_type=F32)
    own_ref[...] = jnp.dot(self_ref[...], grad, preferred_element_type=F32)
    spread = (weight * back.astype(BF16).astype(F32)).astype(BF16)
    contrib = lax.dot_general(
        spread, listed_ref[...], (((1,), (1,)), ((), ())), preferred_element_type=F32
    )
    wgrads = [
        lax.dot_general(x[...], grad, (((1,), (1,)), ((), ())), preferred_element_type=F32)
        for x in (feat_ref, aggs[0])
    ]
    ones = jnp.ones((16, nodes), BF16)
    bias = lax.dot_general(
        ones, cot_full[own_rows, :].astype(BF16), (((1,), (1,)), ((), ())), preferred_element_type=F32
    )[:1]
    high = bias.astype(BF16).astype(F32)
    listed = listed_ref.shape[0] // nodes
    half, short = width // 2, width // LOW
    base = listed * short + half
    for q in range(LOW):
        for r in range(listed):
            wide[q, r * short : (r + 1) * short, :] = contrib[
                q * short : (q + 1) * short, r * nodes : (r + 1) * nodes
            ]
        wide[q, base - half : base, :] = wgrads[q // 2][q % 2 * half : (q % 2 + 1) * half, :]
        wide[q, base:, :] = jnp.zeros((wide.shape[1] - base, nodes), F32)
        wide[q, base : base + 1, :part_h] = high
        wide[q, base + 1 : base + 2, :part_h] = bias - high
    slot_ref[...] = wide[...].astype(BF16)


def group_sum_body(base, got_ref, out_ref, full):
    total = got_ref[0].astype(F32)
    for q in range(1, LOW):
        total += got_ref[q].astype(F32)
    full[...] = total
    bias = total[base : base + 1] + total[base + 1 : base + 2]
    high = bias.astype(BF16).astype(F32)
    full[base : base + 1, :] = high
    full[base + 1 : base + 2, :] = bias - high
    out_ref[...] = full[...].astype(BF16)


def line_sum_body(base, width, count, stale_ref, *refs):
    got, (bias_ref, out_ref, wide, kept, piece, ranks) = refs[:count], refs[count:]
    me = lax.axis_index("dom")
    place = me // LOW
    for m in range(count):
        wide[jnp.bitwise_xor(place, m)] = got[m][...].astype(F32)
    total = wide[0]
    for m in range(1, count):
        total += wide[m]
    bias_ref[...] = jnp.broadcast_to(total[base : base + 1] + total[base + 1 : base + 2], bias_ref.shape)
    half, short = width // 2, width // LOW
    for r in range(kept.shape[0]):
        kept[r] = total[r * short : (r + 1) * short]
    piece[...] = jnp.zeros_like(piece)
    piece[short : short + half, :] = total[base - half : base]
    fill_ranks(stale_ref, ranks)
    for q in range(LOW):
        piece[:short, :] = kept[ranks[place * LOW + q]]
        out_ref[q] = piece[...].astype(BF16)


def last_body(stale_ref, act_ref, bias_ref, own_ref, got_ref, *refs):
    act_out, feat_ref, self_ref, nbr_ref, bias_out, wide, back = refs
    act_out[...] = act_ref[...]
    bias_out[...] = bias_ref[:1, : bias_out.shape[1]]
    width = own_ref.shape[0]
    me = lax.axis_index("dom")
    half, short = width // 2, width // LOW
    wide[...] = got_ref[...].astype(F32)
    fresh = is_fresh(stale_ref, me).astype(F32)
    for q in range(LOW):
        back[q * short : (q + 1) * short, :] = wide[q, :short]
        ref = nbr_ref if q // 2 else self_ref
        ref[q % 2 * half : (q % 2 + 1) * half, :] = wide[q, short : short + half]
    feat_ref[...] = (own_ref[...] + fresh * back[...]).astype(BF16)


def per_device(
    n_col,
    features,
    cached_embed,
    staleness,
    node_counts,
    neighbours,
    degrees,
    w_self,
    w_nbr,
    sage_bias,
    cotangent,
):
    width, nodes = features.shape
    hidden = w_self.shape[1]
    dom = staleness.shape[0]
    listed = dom // 4
    part_h = cotangent.shape[0]
    shape = jax.ShapeDtypeStruct

    def hop(block, m):
        return lax.ppermute(block, "dom", [(i, i ^ m) for i in range(dom)])

    def along(block):
        return [block] + [hop(block, m) for m in range(LOW, dom, LOW)]

    def within(slots):
        return [slots[0]] + [hop(slots[m], m) for m in range(1, LOW)]

    def swap(slots):
        groups = [[g + q for q in range(LOW)] for g in range(0, dom, LOW)]
        return lax.all_to_all(slots, "dom", 0, 0, axis_index_groups=groups, tiled=True)

    def around(block):
        return [
            lax.ppermute(block, "col", [(i, (i + s) % n_col) for i in range(n_col)])
            for s in range(1, n_col)
        ]

    line = along(features)
    bias_row = sage_bias.reshape(1, part_h)
    packed = call(
        pack_body,
        shape((3 * width + part_h + 16, nodes), BF16),
        0,
        0,
        [pltpu.VMEM((1, part_h), F32), pltpu.VMEM((16, nodes), F32), pltpu.SemaphoreType.DMA((5,))],
        moved=4 * (3 * width + part_h) * nodes,
        hbm_count=5,
    )(features, w_self, w_nbr, cotangent, bias_row)
    packs = around(packed)
    deg = degrees.reshape(1, nodes)
    stacked = call(stack_body, shape((width * len(line), nodes), BF16), 0, len(line), moved=4 * dom * width * nodes // LOW)(
        *line
    )
    stacks = within([stacked] * LOW)
    counts, acc, scale = call(
        count_body,
        (shape((listed * nodes, nodes), BF16), shape((width, nodes), F32), shape((16, nodes), F32)),
        2,
        3,
        [pltpu.VMEM((dom * nodes, nodes), BF16)],
        flops=2 * width * dom * nodes * nodes,
        moved=dom * nodes * nodes * 16,
    )(staleness, node_counts, neighbours, deg, cached_embed)
    agg = call(
        mean_body,
        shape((width, nodes), BF16),
        1,
        3 + LOW,
        [pltpu.VMEM((listed, width, nodes), BF16), pltpu.SMEM((dom,), jnp.int32)],
        moved=2 * dom * width * nodes,
    )(staleness, scale, acc, counts, *stacks)
    aggs = [agg] + around(agg)
    base = listed * (width // LOW) + width // 2
    rows = up16(base + 2)
    act, own, slots = call(
        functools.partial(dense_body, n_col),
        [shape((part_h, nodes), BF16), shape((width, nodes), F32), shape((LOW, rows, nodes), BF16)],
        0,
        7 + 2 * n_col - 1,
        [
            pltpu.VMEM((hidden, nodes), F32),
            pltpu.VMEM((hidden, LANES), F32),
            pltpu.VMEM((hidden, nodes), F32),
            pltpu.VMEM((LOW, rows, nodes), F32),
        ],
        flops=2 * width * nodes * (hidden * 6 + listed * nodes),
        moved=4 * LOW * rows * nodes,
    )(scale, counts, features, w_self, w_nbr, bias_row, cotangent, *aggs, *packs)
    summed = call(
        functools.partial(group_sum_body, base),
        shape((rows, nodes), BF16),
        0,
        1,
        [pltpu.VMEM((rows, nodes), F32)],
        moved=2 * LOW * rows * nodes,
    )(swap(slots))
    lines = along(summed)
    tall = up16(width // LOW + width // 2)
    bias, pieces = call(
        functools.partial(line_sum_body, base, width, len(lines)),
        [shape((8, nodes), F32), shape((LOW, tall, nodes), BF16)],
        1,
        len(lines),
        [
            pltpu.VMEM((len(lines), rows, nodes), F32),
            pltpu.VMEM((listed, width // LOW, nodes), F32),
            pltpu.VMEM((tall, nodes), F32),
            pltpu.SMEM((dom,), jnp.int32),
        ],
        moved=2 * len(lines) * rows * nodes,
    )(staleness, *lines)
    act, grad_feat, grad_self, grad_nbr, bias = call(
        last_body,
        (
            shape((part_h, nodes), BF16),
            shape((width, nodes), BF16),
            shape((width, hidden), F32),
            shape((width, hidden), F32),
            shape((1, part_h), F32),
        ),
        1,
        4,
        [pltpu.VMEM((LOW, tall, nodes), F32), pltpu.VMEM((width, nodes), F32)],
        moved=2 * LOW * tall * nodes,
    )(staleness, act, bias, own, swap(pieces))
    return act, grad_feat, grad_self, grad_nbr, bias.reshape(-1)


def solution(mesh):
    placed = (
        P("col", "dom"),
        P("col", None),
        P(),
        P(),
        P(None, "dom"),
        P("dom"),
        P("col", None),
        P("col", None),
        P("col"),
        P("col", "dom"),
    )
    return jax.shard_map(
        functools.partial(per_device, mesh.shape["col"]),
        mesh=mesh,
        in_specs=placed,
        out_specs=(P("col", "dom"), P("col", "dom"), P("col", None), P("col", None), P("col")),
        check_vma=False,
    )
```

```python
import functools

import jax
import jax.numpy as jnp
from jax import lax
from jax.experimental import pallas as pl
from jax.experimental.pallas import tpu as pltpu
from jax.sharding import PartitionSpec as P

LIMIT = 8
LANES = 128
LOW = 4
BF16 = jnp.bfloat16
F32 = jnp.float32
SMEM = pl.BlockSpec(memory_space=pltpu.SMEM)
VMEM = pl.BlockSpec(memory_space=pltpu.VMEM)
HBM = pl.BlockSpec(memory_space=pltpu.HBM)
PARAMS = pltpu.CompilerParams(vmem_limit_bytes=32 * 1024 * 1024)
WHOLE = pltpu.CompilerParams(vmem_limit_bytes=60 * 1024 * 1024)


def call(body, outs, smem_count, vmem_count, scratch=(), flops=0, moved=0, hbm_count=0):
    return pl.pallas_call(
        body,
        out_shape=outs,
        in_specs=[SMEM] * smem_count + [HBM] * hbm_count + [VMEM] * vmem_count,
        out_specs=jax.tree.map(lambda _: VMEM, outs),
        scratch_shapes=list(scratch),
        compiler_params=WHOLE if hbm_count else PARAMS,
        cost_estimate=pl.CostEstimate(flops=flops, bytes_accessed=moved, transcendentals=0),
    )


def up16(rows):
    return -(-rows // 16) * 16


def is_fresh(stale_ref, part):
    return stale_ref[part] >= LIMIT


def fill_ranks(stale_ref, ranks):
    rank = jnp.int32(0)
    for p in range(stale_ref.shape[0]):
        ranks[p] = jnp.minimum(rank, stale_ref.shape[0] // 4 - 1)
        rank += is_fresh(stale_ref, p).astype(jnp.int32)


def split3(x):
    high = x.astype(BF16).astype(F32)
    mid = (x - high).astype(BF16).astype(F32)
    return high, mid, x - high - mid


def count_body(
    stale_ref, counts_ref, nbr_ref, deg_ref, cache_ref, listed_ref, acc_ref, scale_ref, pick_ref, all_ref, ranks
):
    slots, nodes = nbr_ref.shape
    listed = listed_ref.shape[0] // nodes
    used = lax.broadcasted_iota(jnp.int32, (slots, nodes), 0) < deg_ref[...]
    index = jnp.where(used, nbr_ref[...], -1)
    tall = 16
    live = (
        lax.broadcasted_iota(jnp.int32, (1, nodes), 1) < counts_ref[lax.axis_index("dom")]
    ).astype(F32)
    scale_ref[0:8, :] = jnp.broadcast_to(live, (8, nodes))
    scale_ref[8:16, :] = jnp.broadcast_to(live / deg_ref[...].astype(F32), (8, nodes))
    me = lax.axis_index("dom")
    scale_ref[16:24, :] = jnp.full((8, nodes), is_fresh(stale_ref, me).astype(F32))
    fill_ranks(stale_ref, ranks)
    for q in range(LOW):
        place = ranks[me // LOW * LOW + q]
        for r in range(listed):
            pick_ref[q * listed + r : q * listed + r + 1, :] = jnp.full((1, nodes), (place == r).astype(F32))

    def per_part(part, rank):
        fresh = is_fresh(stale_ref, part)
        local = index - part * nodes
        local = jnp.where((local >= 0) & (local < nodes), local, -1).astype(F32)
        rows = [jnp.broadcast_to(local[k : k + 1, :], (tall, nodes)).astype(BF16) for k in range(slots)]
        for top in range(0, nodes, tall):
            place = (lax.broadcasted_iota(jnp.int32, (tall, nodes), 0) + top).astype(F32).astype(BF16)
            total = jnp.zeros((tall, nodes), BF16)
            for k in range(slots):
                total = total + jnp.where(rows[k] == place, BF16(1), BF16(0))
            all_ref[pl.ds(pl.multiple_of(part * nodes + top, tall), tall), :] = total
        block = pl.ds(pl.multiple_of(part * nodes, nodes), nodes)

        @pl.when(fresh)
        def _():
            to = pl.multiple_of(jnp.minimum(rank, listed - 1) * nodes, nodes)
            listed_ref[pl.ds(to, nodes), :] = all_ref[block, :]
            all_ref[block, :] = jnp.zeros((nodes, nodes), BF16)

        return rank + fresh.astype(jnp.int32)

    lax.fori_loop(0, stale_ref.shape[0], per_part, jnp.int32(0))
    acc_ref[...] = jnp.dot(cache_ref[...], all_ref[...], preferred_element_type=F32)


def pack_body(self_ref, nbr_ref, cot_ref, bias_ref, feat_ref, out_ref, bias, wide, sems):
    row = feat_ref.shape[0]
    copies = []
    for i, ref in enumerate((self_ref, nbr_ref, cot_ref)):
        copies.append(pltpu.make_async_copy(ref, out_ref.at[row : row + ref.shape[0], :], sems.at[i]))
        row += ref.shape[0]
    copies.append(pltpu.make_async_copy(bias_ref, bias, sems.at[3]))
    for copy in copies:
        copy.start()
    wide[...] = jnp.zeros_like(wide)
    out_ref[: feat_ref.shape[0], :] = feat_ref[...]
    copies[3].wait()
    for i, term in enumerate(split3(bias[...])):
        wide[i : i + 1, : bias.shape[1]] = term
    out_ref[row:, :] = wide[...].astype(BF16)
    for copy in copies[:3]:
        copy.wait()


def stack_body(*refs):
    ins, out_ref = refs[:-1], refs[-1]
    rows = ins[0].shape[0]
    for i, ref in enumerate(ins):
        out_ref[i * rows : (i + 1) * rows, :] = ref[...]


def mean_body(stale_ref, scale_ref, acc_ref, listed_ref, *refs):
    stacks, (out_ref, blocks, ranks) = refs[:LOW], refs[LOW:]
    width, nodes = acc_ref.shape
    me = lax.axis_index("dom")
    fill_ranks(stale_ref, ranks)
    for low in range(LOW):
        for high in range(stacks[0].shape[0] // width):
            part = jnp.bitwise_xor(me, low + LOW * high)

            @pl.when(is_fresh(stale_ref, part))
            def _(low=low, high=high, part=part):
                blocks[ranks[part]] = stacks[low][high * width : (high + 1) * width, :]

    total = acc_ref[...]
    for r in range(blocks.shape[0]):
        total += jnp.dot(
            blocks[r], listed_ref[r * nodes : (r + 1) * nodes, :], preferred_element_type=F32
        )
    out_ref[...] = (total * scale_ref[8:9, :]).astype(BF16)


def dense_body(n_col, scale_ref, listed_ref, feat_ref, self_ref, nbr_ref, bias_ref, cot_ref, *refs):
    aggs, packs, refs = refs[:n_col], refs[n_col : 2 * n_col - 1], refs[2 * n_col - 1 :]
    act_ref, own_ref, slots, (cot_full, bias_full, full, wide) = refs[0], refs[1], refs[2 : 2 + LOW], refs[2 + LOW :]
    width, nodes = feat_ref.shape
    part_h = cot_ref.shape[0]
    hidden = part_h * n_col
    me = lax.axis_index("col")
    live, weight = scale_ref[0:1, :], scale_ref[8:9, :]
    pre = jnp.zeros((hidden, nodes), F32)
    for s in range(n_col):
        if s == 0:
            feat, w_self, w_nbr, cot, bias = feat_ref[...], self_ref[...], nbr_ref[...], cot_ref[...], bias_ref[...]
        else:
            pack = packs[s - 1]
            feat, w_self, w_nbr = [pack[i * width : (i + 1) * width, :] for i in range(3)]
            cot = pack[3 * width : 3 * width + part_h, :]
            terms = pack[3 * width + part_h :, :].astype(F32)
            bias = (terms[0:1] + terms[1:2] + terms[2:3])[:, :part_h]
        rows = pl.ds(pl.multiple_of(lax.rem(me + n_col - s, n_col) * part_h, part_h), part_h)
        cot_full[rows, :] = cot.astype(F32)
        bias_full[rows, :] = jnp.broadcast_to(bias, (LANES, part_h)).T
        for w, x in ((w_self, feat), (w_nbr, aggs[s][...])):
            pre += jnp.dot(w.astype(F32).T.astype(BF16), x, preferred_element_type=F32)
    pre += jnp.concatenate([bias_full[...]] * (nodes // LANES), 1)
    sig = 1.0 / (1.0 + jnp.exp(-pre))
    full[...] = live * pre * sig
    own_rows = pl.ds(pl.multiple_of(me * part_h, part_h), part_h)
    act_ref[...] = full[own_rows, :].astype(BF16)
    grad = (live * cot_full[...] * sig * (1.0 + pre * (1.0 - sig))).astype(BF16)
    cot_full[...] = grad.astype(F32)
    back = jnp.dot(nbr_ref[...], grad, preferred_element_type=F32)
    own_ref[...] = jnp.dot(self_ref[...], grad, preferred_element_type=F32)
    spread = (weight * back.astype(BF16).astype(F32)).astype(BF16)
    contrib = lax.dot_general(
        spread, listed_ref[...], (((1,), (1,)), ((), ())), preferred_element_type=F32
    )
    wgrads = [
        lax.dot_general(x[...], grad, (((1,), (1,)), ((), ())), preferred_element_type=F32)
        for x in (feat_ref, aggs[0])
    ]
    ones = jnp.ones((16, nodes), BF16)
    bias = lax.dot_general(
        ones, cot_full[own_rows, :].astype(BF16), (((1,), (1,)), ((), ())), preferred_element_type=F32
    )[:1]
    high = bias.astype(BF16).astype(F32)
    listed = listed_ref.shape[0] // nodes
    half, short = width // 2, width // LOW
    base = listed * short + half
    for q in range(LOW):
        for r in range(listed):
            wide[q, r * short : (r + 1) * short, :] = contrib[
                q * short : (q + 1) * short, r * nodes : (r + 1) * nodes
            ]
        wide[q, base - half : base, :] = wgrads[q // 2][q % 2 * half : (q % 2 + 1) * half, :]
        wide[q, base:, :] = jnp.zeros((wide.shape[1] - base, nodes), F32)
        wide[q, base : base + 1, :part_h] = high
        wide[q, base + 1 : base + 2, :part_h] = bias - high
    low = lax.axis_index("dom") % LOW
    for m in range(LOW):
        slots[m][...] = wide[jnp.bitwise_xor(low, m)].astype(BF16)


def group_sum_body(base, *refs):
    got, (out_ref, wide, full) = refs[:LOW], refs[LOW:]
    low = lax.axis_index("dom") % LOW
    for m in range(LOW):
        wide[jnp.bitwise_xor(low, m)] = got[m][...].astype(F32)
    total = wide[0] + wide[1] + wide[2] + wide[3]
    full[...] = total
    bias = total[base : base + 1] + total[base + 1 : base + 2]
    high = bias.astype(BF16).astype(F32)
    full[base : base + 1, :] = high
    full[base + 1 : base + 2, :] = bias - high
    out_ref[...] = full[...].astype(BF16)


def line_sum_body(base, width, count, pick_ref, *refs):
    got, bias_ref, outs = refs[:count], refs[count], refs[count + 1 : count + 1 + LOW]
    wide, piece, pieces = refs[count + 1 + LOW :]
    me = lax.axis_index("dom")
    place = me // LOW
    for m in range(count):
        wide[jnp.bitwise_xor(place, m)] = got[m][...].astype(F32)
    total = wide[0]
    for m in range(1, count):
        total += wide[m]
    bias_ref[...] = jnp.broadcast_to(total[base : base + 1] + total[base + 1 : base + 2], bias_ref.shape)
    half, short = width // 2, width // LOW
    piece[...] = jnp.zeros_like(piece)
    piece[short : short + half, :] = total[base - half : base]
    listed = pick_ref.shape[0] // LOW
    for q in range(LOW):
        mine = jnp.zeros((short, total.shape[1]), F32)
        for r in range(listed):
            row = q * listed + r
            mine += pick_ref[row : row + 1, :] * total[r * short : (r + 1) * short]
        piece[:short, :] = mine
        pieces[q] = piece[...]
    for m in range(LOW):
        outs[m][...] = pieces[jnp.bitwise_xor(me % LOW, m)].astype(BF16)


def last_body(scale_ref, act_ref, bias_ref, own_ref, *refs):
    got, (act_out, feat_ref, self_ref, nbr_ref, bias_out, wide, back) = refs[:LOW], refs[LOW:]
    act_out[...] = act_ref[...]
    bias_out[...] = bias_ref[:1, : bias_out.shape[1]]
    width = own_ref.shape[0]
    me = lax.axis_index("dom")
    low = me % LOW
    half, short = width // 2, width // LOW
    for m in range(LOW):
        wide[jnp.bitwise_xor(low, m)] = got[m][...].astype(F32)
    fresh = scale_ref[16:17, :]
    for q in range(LOW):
        back[q * short : (q + 1) * short, :] = wide[q, :short]
        ref = nbr_ref if q // 2 else self_ref
        ref[q % 2 * half : (q % 2 + 1) * half, :] = wide[q, short : short + half]
    feat_ref[...] = (own_ref[...] + fresh * back[...]).astype(BF16)


def per_device(
    n_col,
    features,
    cached_embed,
    staleness,
    node_counts,
    neighbours,
    degrees,
    w_self,
    w_nbr,
    sage_bias,
    cotangent,
):
    width, nodes = features.shape
    hidden = w_self.shape[1]
    dom = staleness.shape[0]
    listed = dom // 4
    part_h = cotangent.shape[0]
    shape = jax.ShapeDtypeStruct

    def hop(block, m):
        return lax.ppermute(block, "dom", [(i, i ^ m) for i in range(dom)])

    def along(block):
        return [block] + [hop(block, m) for m in range(LOW, dom, LOW)]

    def within(slots):
        return [slots[0]] + [hop(slots[m], m) for m in range(1, LOW)]

    def around(block):
        return [
            lax.ppermute(block, "col", [(i, (i + s) % n_col) for i in range(n_col)])
            for s in range(1, n_col)
        ]

    line = along(features)
    bias_row = sage_bias.reshape(1, part_h)
    packed = call(
        pack_body,
        shape((3 * width + part_h + 16, nodes), BF16),
        0,
        1,
        [pltpu.VMEM((1, part_h), F32), pltpu.VMEM((16, nodes), F32), pltpu.SemaphoreType.DMA((4,))],
        moved=4 * (3 * width + part_h) * nodes,
        hbm_count=4,
    )(w_self, w_nbr, cotangent, bias_row, features)
    packs = around(packed)
    deg = degrees.reshape(1, nodes)
    stacked = call(stack_body, shape((width * len(line), nodes), BF16), 0, len(line), moved=4 * dom * width * nodes // LOW)(
        *line
    )
    stacks = within([stacked] * LOW)
    counts, acc, scale, picks = call(
        count_body,
        (
            shape((listed * nodes, nodes), BF16),
            shape((width, nodes), F32),
            shape((24, nodes), F32),
            shape((LOW * listed, nodes), F32),
        ),
        2,
        3,
        [pltpu.VMEM((dom * nodes, nodes), BF16), pltpu.SMEM((dom,), jnp.int32)],
        flops=2 * width * dom * nodes * nodes,
        moved=dom * nodes * nodes * 16,
    )(staleness, node_counts, neighbours, deg, cached_embed)
    agg = call(
        mean_body,
        shape((width, nodes), BF16),
        1,
        3 + LOW,
        [pltpu.VMEM((listed, width, nodes), BF16), pltpu.SMEM((dom,), jnp.int32)],
        moved=2 * dom * width * nodes,
    )(staleness, scale, acc, counts, *stacks)
    aggs = [agg] + around(agg)
    base = listed * (width // LOW) + width // 2
    rows = up16(base + 2)
    act, own, *slots = call(
        functools.partial(dense_body, n_col),
        [shape((part_h, nodes), BF16), shape((width, nodes), F32)] + [shape((rows, nodes), BF16)] * LOW,
        0,
        7 + 2 * n_col - 1,
        [
            pltpu.VMEM((hidden, nodes), F32),
            pltpu.VMEM((hidden, LANES), F32),
            pltpu.VMEM((hidden, nodes), F32),
            pltpu.VMEM((LOW, rows, nodes), F32),
        ],
        flops=2 * width * nodes * (hidden * 6 + listed * nodes),
        moved=4 * LOW * rows * nodes,
    )(scale, counts, features, w_self, w_nbr, bias_row, cotangent, *aggs, *packs)
    summed = call(
        functools.partial(group_sum_body, base),
        shape((rows, nodes), BF16),
        0,
        LOW,
        [pltpu.VMEM((LOW, rows, nodes), F32), pltpu.VMEM((rows, nodes), F32)],
        moved=2 * LOW * rows * nodes,
    )(*within(slots))
    lines = along(summed)
    tall = up16(width // LOW + width // 2)
    bias, *pieces = call(
        functools.partial(line_sum_body, base, width, len(lines)),
        [shape((8, nodes), F32)] + [shape((tall, nodes), BF16)] * LOW,
        0,
        1 + len(lines),
        [
            pltpu.VMEM((len(lines), rows, nodes), F32),
            pltpu.VMEM((tall, nodes), F32),
            pltpu.VMEM((LOW, tall, nodes), F32),
        ],
        moved=2 * len(lines) * rows * nodes,
    )(picks, *lines)
    act, grad_feat, grad_self, grad_nbr, bias = call(
        last_body,
        (
            shape((part_h, nodes), BF16),
            shape((width, nodes), BF16),
            shape((width, hidden), F32),
            shape((width, hidden), F32),
            shape((1, part_h), F32),
        ),
        0,
        4 + LOW,
        [pltpu.VMEM((LOW, tall, nodes), F32), pltpu.VMEM((width, nodes), F32)],
        moved=2 * LOW * tall * nodes,
    )(scale, act, bias, own, *within(pieces))
    return act, grad_feat, grad_self, grad_nbr, bias.reshape(-1)


def solution(mesh):
    placed = (
        P("col", "dom"),
        P("col", None),
        P(),
        P(),
        P(None, "dom"),
        P("dom"),
        P("col", None),
        P("col", None),
        P("col"),
        P("col", "dom"),
    )
    return jax.shard_map(
        functools.partial(per_device, mesh.shape["col"]),
        mesh=mesh,
        in_specs=placed,
        out_specs=(P("col", "dom"), P("col", "dom"), P("col", None), P("col", None), P("col")),
        check_vma=False,
    )
```

```python
import functools

import jax
import jax.numpy as jnp
from jax import lax
from jax.experimental import pallas as pl
from jax.experimental.pallas import tpu as pltpu
from jax.sharding import PartitionSpec as P

LIMIT = 8
LANES = 128
LOW = 4
BF16 = jnp.bfloat16
F32 = jnp.float32
SMEM = pl.BlockSpec(memory_space=pltpu.SMEM)
VMEM = pl.BlockSpec(memory_space=pltpu.VMEM)
HBM = pl.BlockSpec(memory_space=pltpu.HBM)
PARAMS = pltpu.CompilerParams(vmem_limit_bytes=32 * 1024 * 1024)
WHOLE = pltpu.CompilerParams(vmem_limit_bytes=60 * 1024 * 1024)


def call(body, outs, smem_count, vmem_count, scratch=(), flops=0, moved=0, hbm_count=0):
    return pl.pallas_call(
        body,
        out_shape=outs,
        in_specs=[SMEM] * smem_count + [HBM] * hbm_count + [VMEM] * vmem_count,
        out_specs=jax.tree.map(lambda _: VMEM, outs),
        scratch_shapes=list(scratch),
        compiler_params=WHOLE if hbm_count else PARAMS,
        cost_estimate=pl.CostEstimate(flops=flops, bytes_accessed=moved, transcendentals=0),
    )


def up16(rows):
    return -(-rows // 16) * 16


def is_fresh(stale_ref, part):
    return stale_ref[part] >= LIMIT


def fill_ranks(stale_ref, ranks):
    rank = jnp.int32(0)
    for p in range(stale_ref.shape[0]):
        ranks[p] = jnp.minimum(rank, stale_ref.shape[0] // 4 - 1)
        rank += is_fresh(stale_ref, p).astype(jnp.int32)


def split3(x):
    high = x.astype(BF16).astype(F32)
    mid = (x - high).astype(BF16).astype(F32)
    return high, mid, x - high - mid


def count_body(
    stale_ref, counts_ref, nbr_ref, deg_ref, cache_ref, listed_ref, acc_ref, scale_ref, pick_ref, find_ref, all_ref, ranks
):
    slots, nodes = nbr_ref.shape
    listed = listed_ref.shape[0] // nodes
    used = lax.broadcasted_iota(jnp.int32, (slots, nodes), 0) < deg_ref[...]
    index = jnp.where(used, nbr_ref[...], -1)
    tall = 16
    live = (
        lax.broadcasted_iota(jnp.int32, (1, nodes), 1) < counts_ref[lax.axis_index("dom")]
    ).astype(F32)
    scale_ref[0:8, :] = jnp.broadcast_to(live, (8, nodes))
    scale_ref[8:16, :] = jnp.broadcast_to(live / deg_ref[...].astype(F32), (8, nodes))
    me = lax.axis_index("dom")
    scale_ref[16:24, :] = jnp.full((8, nodes), is_fresh(stale_ref, me).astype(F32))
    fill_ranks(stale_ref, ranks)
    for m in range(stale_ref.shape[0]):
        part = jnp.bitwise_xor(me, m)
        place = jnp.where(is_fresh(stale_ref, part), ranks[part], -1)
        for r in range(listed):
            row = r * stale_ref.shape[0] + m
            find_ref[row : row + 1, :] = jnp.full((1, nodes), (place == r).astype(F32))
    for q in range(LOW):
        place = ranks[me // LOW * LOW + q]
        for r in range(listed):
            pick_ref[q * listed + r : q * listed + r + 1, :] = jnp.full((1, nodes), (place == r).astype(F32))

    def per_part(part, rank):
        fresh = is_fresh(stale_ref, part)
        local = index - part * nodes
        local = jnp.where((local >= 0) & (local < nodes), local, -1).astype(F32)
        rows = [jnp.broadcast_to(local[k : k + 1, :], (tall, nodes)).astype(BF16) for k in range(slots)]
        for top in range(0, nodes, tall):
            place = (lax.broadcasted_iota(jnp.int32, (tall, nodes), 0) + top).astype(F32).astype(BF16)
            total = jnp.zeros((tall, nodes), BF16)
            for k in range(slots):
                total = total + jnp.where(rows[k] == place, BF16(1), BF16(0))
            all_ref[pl.ds(pl.multiple_of(part * nodes + top, tall), tall), :] = total
        block = pl.ds(pl.multiple_of(part * nodes, nodes), nodes)

        @pl.when(fresh)
        def _():
            to = pl.multiple_of(jnp.minimum(rank, listed - 1) * nodes, nodes)
            listed_ref[pl.ds(to, nodes), :] = all_ref[block, :]
            all_ref[block, :] = jnp.zeros((nodes, nodes), BF16)

        return rank + fresh.astype(jnp.int32)

    lax.fori_loop(0, stale_ref.shape[0], per_part, jnp.int32(0))
    acc_ref[...] = jnp.dot(cache_ref[...], all_ref[...], preferred_element_type=F32)


def pack_body(feat_ref, self_ref, nbr_ref, cot_ref, bias_ref, out_ref, bias, wide, sems):
    row = 0
    copies = []
    for i, ref in enumerate((feat_ref, self_ref, nbr_ref, cot_ref)):
        copies.append(pltpu.make_async_copy(ref, out_ref.at[row : row + ref.shape[0], :], sems.at[i]))
        row += ref.shape[0]
    copies.append(pltpu.make_async_copy(bias_ref, bias, sems.at[4]))
    for copy in copies:
        copy.start()
    wide[...] = jnp.zeros_like(wide)
    copies[4].wait()
    for i, term in enumerate(split3(bias[...])):
        wide[i : i + 1, : bias.shape[1]] = term
    out_ref[row:, :] = wide[...].astype(BF16)
    for copy in copies[:4]:
        copy.wait()


def stack_body(*refs):
    ins, out_ref = refs[:-1], refs[-1]
    rows = ins[0].shape[0]
    for i, ref in enumerate(ins):
        out_ref[i * rows : (i + 1) * rows, :] = ref[...]


def mean_body(find_ref, scale_ref, acc_ref, listed_ref, *refs):
    stacks, out_ref = refs[:LOW], refs[LOW]
    width, nodes = acc_ref.shape
    listed = listed_ref.shape[0] // nodes
    dom = find_ref.shape[0] // listed
    total = acc_ref[...]
    for r in range(listed):
        block = jnp.zeros((width // 16, 16, nodes), BF16)
        for m in range(dom):
            row = r * dom + m
            one = jnp.broadcast_to(find_ref[row : row + 1, :], (16, nodes)).astype(BF16)
            low, high = m % LOW, m // LOW
            part = stacks[low][high * width : (high + 1) * width, :].reshape(width // 16, 16, nodes)
            block = block + part * one[None]
        total += jnp.dot(
            block.reshape(width, nodes),
            listed_ref[r * nodes : (r + 1) * nodes, :],
            preferred_element_type=F32,
        )
    out_ref[...] = (total * scale_ref[8:9, :]).astype(BF16)


def dense_body(n_col, scale_ref, listed_ref, feat_ref, self_ref, nbr_ref, bias_ref, cot_ref, *refs):
    aggs, packs, refs = refs[:n_col], refs[n_col : 2 * n_col - 1], refs[2 * n_col - 1 :]
    act_ref, own_ref, slots, (cot_full, bias_full, full, wide) = refs[0], refs[1], refs[2 : 2 + LOW], refs[2 + LOW :]
    width, nodes = feat_ref.shape
    part_h = cot_ref.shape[0]
    hidden = part_h * n_col
    me = lax.axis_index("col")
    live, weight = scale_ref[0:1, :], scale_ref[8:9, :]
    pre = jnp.zeros((hidden, nodes), F32)
    for s in range(n_col):
        if s == 0:
            feat, w_self, w_nbr, cot, bias = feat_ref[...], self_ref[...], nbr_ref[...], cot_ref[...], bias_ref[...]
        else:
            pack = packs[s - 1]
            feat, w_self, w_nbr = [pack[i * width : (i + 1) * width, :] for i in range(3)]
            cot = pack[3 * width : 3 * width + part_h, :]
            terms = pack[3 * width + part_h :, :].astype(F32)
            bias = (terms[0:1] + terms[1:2] + terms[2:3])[:, :part_h]
        rows = pl.ds(pl.multiple_of(lax.rem(me + n_col - s, n_col) * part_h, part_h), part_h)
        cot_full[rows, :] = cot.astype(F32)
        bias_full[rows, :] = jnp.broadcast_to(bias, (LANES, part_h)).T
        for w, x in ((w_self, feat), (w_nbr, aggs[s][...])):
            pre += jnp.dot(w.astype(F32).T.astype(BF16), x, preferred_element_type=F32)
    pre += jnp.concatenate([bias_full[...]] * (nodes // LANES), 1)
    sig = 1.0 / (1.0 + jnp.exp(-pre))
    full[...] = live * pre * sig
    own_rows = pl.ds(pl.multiple_of(me * part_h, part_h), part_h)
    act_ref[...] = full[own_rows, :].astype(BF16)
    grad = (live * cot_full[...] * sig * (1.0 + pre * (1.0 - sig))).astype(BF16)
    cot_full[...] = grad.astype(F32)
    back = jnp.dot(nbr_ref[...], grad, preferred_element_type=F32)
    own_ref[...] = jnp.dot(self_ref[...], grad, preferred_element_type=F32)
    spread = (weight * back.astype(BF16).astype(F32)).astype(BF16)
    contrib = lax.dot_general(
        spread, listed_ref[...], (((1,), (1,)), ((), ())), preferred_element_type=F32
    )
    wgrads = [
        lax.dot_general(x[...], grad, (((1,), (1,)), ((), ())), preferred_element_type=F32)
        for x in (feat_ref, aggs[0])
    ]
    ones = jnp.ones((16, nodes), BF16)
    bias = lax.dot_general(
        ones, cot_full[own_rows, :].astype(BF16), (((1,), (1,)), ((), ())), preferred_element_type=F32
    )[:1]
    high = bias.astype(BF16).astype(F32)
    listed = listed_ref.shape[0] // nodes
    half, short = width // 2, width // LOW
    base = listed * short + half
    for q in range(LOW):
        for r in range(listed):
            wide[q, r * short : (r + 1) * short, :] = contrib[
                q * short : (q + 1) * short, r * nodes : (r + 1) * nodes
            ]
        wide[q, base - half : base, :] = wgrads[q // 2][q % 2 * half : (q % 2 + 1) * half, :]
        wide[q, base:, :] = jnp.zeros((wide.shape[1] - base, nodes), F32)
        wide[q, base : base + 1, :part_h] = high
        wide[q, base + 1 : base + 2, :part_h] = bias - high
    low = lax.axis_index("dom") % LOW
    for m in range(LOW):
        slots[m][...] = wide[jnp.bitwise_xor(low, m)].astype(BF16)


def group_sum_body(base, *refs):
    got, (out_ref, wide, full) = refs[:LOW], refs[LOW:]
    low = lax.axis_index("dom") % LOW
    for m in range(LOW):
        wide[jnp.bitwise_xor(low, m)] = got[m][...].astype(F32)
    total = wide[0] + wide[1] + wide[2] + wide[3]
    full[...] = total
    bias = total[base : base + 1] + total[base + 1 : base + 2]
    high = bias.astype(BF16).astype(F32)
    full[base : base + 1, :] = high
    full[base + 1 : base + 2, :] = bias - high
    out_ref[...] = full[...].astype(BF16)


def line_sum_body(base, width, count, pick_ref, *refs):
    got, bias_ref, outs = refs[:count], refs[count], refs[count + 1 : count + 1 + LOW]
    wide, piece, pieces = refs[count + 1 + LOW :]
    me = lax.axis_index("dom")
    place = me // LOW
    for m in range(count):
        wide[jnp.bitwise_xor(place, m)] = got[m][...].astype(F32)
    total = wide[0]
    for m in range(1, count):
        total += wide[m]
    bias_ref[...] = jnp.broadcast_to(total[base : base + 1] + total[base + 1 : base + 2], bias_ref.shape)
    half, short = width // 2, width // LOW
    piece[...] = jnp.zeros_like(piece)
    piece[short : short + half, :] = total[base - half : base]
    listed = pick_ref.shape[0] // LOW
    for q in range(LOW):
        mine = jnp.zeros((short, total.shape[1]), F32)
        for r in range(listed):
            row = q * listed + r
            mine += pick_ref[row : row + 1, :] * total[r * short : (r + 1) * short]
        piece[:short, :] = mine
        pieces[q] = piece[...]
    for m in range(LOW):
        outs[m][...] = pieces[jnp.bitwise_xor(me % LOW, m)].astype(BF16)


def last_body(scale_ref, act_ref, bias_ref, own_ref, *refs):
    got, (act_out, feat_ref, self_ref, nbr_ref, bias_out, wide, back) = refs[:LOW], refs[LOW:]
    act_out[...] = act_ref[...]
    bias_out[...] = bias_ref[:1, : bias_out.shape[1]]
    width = own_ref.shape[0]
    me = lax.axis_index("dom")
    low = me % LOW
    half, short = width // 2, width // LOW
    for m in range(LOW):
        wide[jnp.bitwise_xor(low, m)] = got[m][...].astype(F32)
    fresh = scale_ref[16:17, :]
    for q in range(LOW):
        back[q * short : (q + 1) * short, :] = wide[q, :short]
        ref = nbr_ref if q // 2 else self_ref
        ref[q % 2 * half : (q % 2 + 1) * half, :] = wide[q, short : short + half]
    feat_ref[...] = (own_ref[...] + fresh * back[...]).astype(BF16)


def per_device(
    n_col,
    features,
    cached_embed,
    staleness,
    node_counts,
    neighbours,
    degrees,
    w_self,
    w_nbr,
    sage_bias,
    cotangent,
):
    width, nodes = features.shape
    hidden = w_self.shape[1]
    dom = staleness.shape[0]
    listed = dom // 4
    part_h = cotangent.shape[0]
    shape = jax.ShapeDtypeStruct

    def hop(block, m):
        return lax.ppermute(block, "dom", [(i, i ^ m) for i in range(dom)])

    def along(block):
        return [block] + [hop(block, m) for m in range(LOW, dom, LOW)]

    def within(slots):
        return [slots[0]] + [hop(slots[m], m) for m in range(1, LOW)]

    def around(block):
        return [
            lax.ppermute(block, "col", [(i, (i + s) % n_col) for i in range(n_col)])
            for s in range(1, n_col)
        ]

    line = along(features)
    bias_row = sage_bias.reshape(1, part_h)
    packed = call(
        pack_body,
        shape((3 * width + part_h + 16, nodes), BF16),
        0,
        0,
        [pltpu.VMEM((1, part_h), F32), pltpu.VMEM((16, nodes), F32), pltpu.SemaphoreType.DMA((5,))],
        moved=4 * (3 * width + part_h) * nodes,
        hbm_count=5,
    )(features, w_self, w_nbr, cotangent, bias_row)
    packs = around(packed)
    deg = degrees.reshape(1, nodes)
    stacked = call(stack_body, shape((width * len(line), nodes), BF16), 0, len(line), moved=4 * dom * width * nodes // LOW)(
        *line
    )
    stacks = within([stacked] * LOW)
    counts, acc, scale, picks, finds = call(
        count_body,
        (
            shape((listed * nodes, nodes), BF16),
            shape((width, nodes), F32),
            shape((24, nodes), F32),
            shape((LOW * listed, nodes), F32),
            shape((dom * listed, nodes), F32),
        ),
        2,
        3,
        [pltpu.VMEM((dom * nodes, nodes), BF16), pltpu.SMEM((dom,), jnp.int32)],
        flops=2 * width * dom * nodes * nodes,
        moved=dom * nodes * nodes * 16,
    )(staleness, node_counts, neighbours, deg, cached_embed)
    agg = call(
        mean_body,
        shape((width, nodes), BF16),
        0,
        4 + LOW,
        moved=2 * dom * width * nodes,
    )(finds, scale, acc, counts, *stacks)
    aggs = [agg] + around(agg)
    base = listed * (width // LOW) + width // 2
    rows = up16(base + 2)
    act, own, *slots = call(
        functools.partial(dense_body, n_col),
        [shape((part_h, nodes), BF16), shape((width, nodes), F32)] + [shape((rows, nodes), BF16)] * LOW,
        0,
        7 + 2 * n_col - 1,
        [
            pltpu.VMEM((hidden, nodes), F32),
            pltpu.VMEM((hidden, LANES), F32),
            pltpu.VMEM((hidden, nodes), F32),
            pltpu.VMEM((LOW, rows, nodes), F32),
        ],
        flops=2 * width * nodes * (hidden * 6 + listed * nodes),
        moved=4 * LOW * rows * nodes,
    )(scale, counts, features, w_self, w_nbr, bias_row, cotangent, *aggs, *packs)
    summed = call(
        functools.partial(group_sum_body, base),
        shape((rows, nodes), BF16),
        0,
        LOW,
        [pltpu.VMEM((LOW, rows, nodes), F32), pltpu.VMEM((rows, nodes), F32)],
        moved=2 * LOW * rows * nodes,
    )(*within(slots))
    lines = along(summed)
    tall = up16(width // LOW + width // 2)
    bias, *pieces = call(
        functools.partial(line_sum_body, base, width, len(lines)),
        [shape((8, nodes), F32)] + [shape((tall, nodes), BF16)] * LOW,
        0,
        1 + len(lines),
        [
            pltpu.VMEM((len(lines), rows, nodes), F32),
            pltpu.VMEM((tall, nodes), F32),
            pltpu.VMEM((LOW, tall, nodes), F32),
        ],
        moved=2 * len(lines) * rows * nodes,
    )(picks, *lines)
    act, grad_feat, grad_self, grad_nbr, bias = call(
        last_body,
        (
            shape((part_h, nodes), BF16),
            shape((width, nodes), BF16),
            shape((width, hidden), F32),
            shape((width, hidden), F32),
            shape((1, part_h), F32),
        ),
        0,
        4 + LOW,
        [pltpu.VMEM((LOW, tall, nodes), F32), pltpu.VMEM((width, nodes), F32)],
        moved=2 * LOW * tall * nodes,
    )(scale, act, bias, own, *within(pieces))
    return act, grad_feat, grad_self, grad_nbr, bias.reshape(-1)


def solution(mesh):
    placed = (
        P("col", "dom"),
        P("col", None),
        P(),
        P(),
        P(None, "dom"),
        P("dom"),
        P("col", None),
        P("col", None),
        P("col"),
        P("col", "dom"),
    )
    return jax.shard_map(
        functools.partial(per_device, mesh.shape["col"]),
        mesh=mesh,
        in_specs=placed,
        out_specs=(P("col", "dom"), P("col", "dom"), P("col", None), P("col", None), P("col")),
        check_vma=False,
    )
```

```python
import functools

import jax
import jax.numpy as jnp
from jax import lax
from jax.experimental import pallas as pl
from jax.experimental.pallas import tpu as pltpu
from jax.sharding import PartitionSpec as P

LIMIT = 8
LANES = 128
LOW = 4
BF16 = jnp.bfloat16
F32 = jnp.float32
SMEM = pl.BlockSpec(memory_space=pltpu.SMEM)
VMEM = pl.BlockSpec(memory_space=pltpu.VMEM)
HBM = pl.BlockSpec(memory_space=pltpu.HBM)
PARAMS = pltpu.CompilerParams(vmem_limit_bytes=32 * 1024 * 1024)
WHOLE = pltpu.CompilerParams(vmem_limit_bytes=60 * 1024 * 1024)


def call(body, outs, smem_count, vmem_count, scratch=(), flops=0, moved=0, hbm_count=0):
    return pl.pallas_call(
        body,
        out_shape=outs,
        in_specs=[SMEM] * smem_count + [HBM] * hbm_count + [VMEM] * vmem_count,
        out_specs=jax.tree.map(lambda _: VMEM, outs),
        scratch_shapes=list(scratch),
        compiler_params=WHOLE if hbm_count else PARAMS,
        cost_estimate=pl.CostEstimate(flops=flops, bytes_accessed=moved, transcendentals=0),
    )


def up16(rows):
    return -(-rows // 16) * 16


def is_fresh(stale_ref, part):
    return stale_ref[part] >= LIMIT


def fill_ranks(stale_ref, ranks):
    rank = jnp.int32(0)
    for p in range(stale_ref.shape[0]):
        ranks[p] = jnp.minimum(rank, stale_ref.shape[0] // 4 - 1)
        rank += is_fresh(stale_ref, p).astype(jnp.int32)


def split3(x):
    high = x.astype(BF16).astype(F32)
    mid = (x - high).astype(BF16).astype(F32)
    return high, mid, x - high - mid


def count_body(
    stale_ref, counts_ref, nbr_ref, deg_ref, cache_ref, listed_ref, acc_ref, scale_ref, pick_ref, find_ref, all_ref, ranks
):
    slots, nodes = nbr_ref.shape
    listed = listed_ref.shape[0] // nodes
    used = lax.broadcasted_iota(jnp.int32, (slots, nodes), 0) < deg_ref[...]
    index = jnp.where(used, nbr_ref[...], -1)
    tall = 16
    live = (
        lax.broadcasted_iota(jnp.int32, (1, nodes), 1) < counts_ref[lax.axis_index("dom")]
    ).astype(F32)
    scale_ref[0:8, :] = jnp.broadcast_to(live, (8, nodes))
    scale_ref[8:16, :] = jnp.broadcast_to(live / deg_ref[...].astype(F32), (8, nodes))
    me = lax.axis_index("dom")
    scale_ref[16:24, :] = jnp.full((8, nodes), is_fresh(stale_ref, me).astype(F32))
    fill_ranks(stale_ref, ranks)
    for m in range(stale_ref.shape[0]):
        part = jnp.bitwise_xor(me, m)
        place = jnp.where(is_fresh(stale_ref, part), ranks[part], -1)
        for r in range(listed):
            row = r * stale_ref.shape[0] + m
            find_ref[row : row + 1, :] = jnp.full((1, nodes), (place == r).astype(F32))
    for q in range(LOW):
        place = ranks[me // LOW * LOW + q]
        for r in range(listed):
            pick_ref[q * listed + r : q * listed + r + 1, :] = jnp.full((1, nodes), (place == r).astype(F32))

    def per_part(part, rank):
        fresh = is_fresh(stale_ref, part)
        local = index - part * nodes
        local = jnp.where((local >= 0) & (local < nodes), local, -1).astype(F32)
        rows = [jnp.broadcast_to(local[k : k + 1, :], (tall, nodes)).astype(BF16) for k in range(slots)]
        for top in range(0, nodes, tall):
            place = (lax.broadcasted_iota(jnp.int32, (tall, nodes), 0) + top).astype(F32).astype(BF16)
            total = jnp.zeros((tall, nodes), BF16)
            for k in range(slots):
                total = total + jnp.where(rows[k] == place, BF16(1), BF16(0))
            all_ref[pl.ds(pl.multiple_of(part * nodes + top, tall), tall), :] = total
        block = pl.ds(pl.multiple_of(part * nodes, nodes), nodes)

        @pl.when(fresh)
        def _():
            to = pl.multiple_of(jnp.minimum(rank, listed - 1) * nodes, nodes)
            listed_ref[pl.ds(to, nodes), :] = all_ref[block, :]
            all_ref[block, :] = jnp.zeros((nodes, nodes), BF16)

        return rank + fresh.astype(jnp.int32)

    lax.fori_loop(0, stale_ref.shape[0], per_part, jnp.int32(0))
    acc_ref[...] = jnp.dot(cache_ref[...], all_ref[...], preferred_element_type=F32)


def pack_body(feat_ref, self_ref, nbr_ref, cot_ref, bias_ref, out_ref, bias, wide, sems):
    row = 0
    copies = []
    for i, ref in enumerate((feat_ref, self_ref, nbr_ref, cot_ref)):
        copies.append(pltpu.make_async_copy(ref, out_ref.at[row : row + ref.shape[0], :], sems.at[i]))
        row += ref.shape[0]
    copies.append(pltpu.make_async_copy(bias_ref, bias, sems.at[4]))
    for copy in copies:
        copy.start()
    wide[...] = jnp.zeros_like(wide)
    copies[4].wait()
    for i, term in enumerate(split3(bias[...])):
        wide[i : i + 1, : bias.shape[1]] = term
    out_ref[row:, :] = wide[...].astype(BF16)
    for copy in copies[:4]:
        copy.wait()


def stack_body(*refs):
    ins, out_ref = refs[:-1], refs[-1]
    rows = ins[0].shape[0]
    for i, ref in enumerate(ins):
        out_ref[i * rows : (i + 1) * rows, :] = ref[...]


def mean_body(find_ref, scale_ref, acc_ref, listed_ref, *refs):
    stacks, out_ref = refs[:LOW], refs[LOW]
    width, nodes = acc_ref.shape
    listed = listed_ref.shape[0] // nodes
    dom = find_ref.shape[0] // listed
    total = acc_ref[...]
    for r in range(listed):
        block = jnp.zeros((width // 16, 16, nodes), BF16)
        for m in range(dom):
            row = r * dom + m
            one = jnp.broadcast_to(find_ref[row : row + 1, :], (16, nodes)).astype(BF16)
            low, high = m % LOW, m // LOW
            part = stacks[low][high * width : (high + 1) * width, :].reshape(width // 16, 16, nodes)
            block = block + part * one[None]
        total += jnp.dot(
            block.reshape(width, nodes),
            listed_ref[r * nodes : (r + 1) * nodes, :],
            preferred_element_type=F32,
        )
    out_ref[...] = (total * scale_ref[8:9, :]).astype(BF16)


def dense_body(n_col, scale_ref, listed_ref, feat_ref, self_ref, nbr_ref, bias_ref, cot_ref, *refs):
    aggs, packs, refs = refs[:n_col], refs[n_col : 2 * n_col - 1], refs[2 * n_col - 1 :]
    act_ref, own_ref, slots, (cot_full, bias_full, full, wide) = refs[0], refs[1], refs[2 : 2 + LOW], refs[2 + LOW :]
    width, nodes = feat_ref.shape
    part_h = cot_ref.shape[0]
    hidden = part_h * n_col
    me = lax.axis_index("col")
    live, weight = scale_ref[0:1, :], scale_ref[8:9, :]
    pre = jnp.zeros((hidden, nodes), F32)
    for s in range(n_col):
        if s == 0:
            feat, w_self, w_nbr, cot, bias = feat_ref[...], self_ref[...], nbr_ref[...], cot_ref[...], bias_ref[...]
        else:
            pack = packs[s - 1]
            feat, w_self, w_nbr = [pack[i * width : (i + 1) * width, :] for i in range(3)]
            cot = pack[3 * width : 3 * width + part_h, :]
            terms = pack[3 * width + part_h :, :].astype(F32)
            bias = (terms[0:1] + terms[1:2] + terms[2:3])[:, :part_h]
        rows = pl.ds(pl.multiple_of(lax.rem(me + n_col - s, n_col) * part_h, part_h), part_h)
        cot_full[rows, :] = cot.astype(F32)
        bias_full[rows, :] = jnp.broadcast_to(bias, (LANES, part_h)).T
        for w, x in ((w_self, feat), (w_nbr, aggs[s][...])):
            pre += jnp.dot(w.astype(F32).T.astype(BF16), x, preferred_element_type=F32)
    pre += jnp.concatenate([bias_full[...]] * (nodes // LANES), 1)
    sig = 1.0 / (1.0 + jnp.exp(-pre))
    full[...] = live * pre * sig
    own_rows = pl.ds(pl.multiple_of(me * part_h, part_h), part_h)
    act_ref[...] = full[own_rows, :].astype(BF16)
    grad = (live * cot_full[...] * sig * (1.0 + pre * (1.0 - sig))).astype(BF16)
    cot_full[...] = grad.astype(F32)
    back = jnp.dot(nbr_ref[...], grad, preferred_element_type=F32)
    own_ref[...] = jnp.dot(self_ref[...], grad, preferred_element_type=F32)
    spread = (weight * back.astype(BF16).astype(F32)).astype(BF16)
    contrib = lax.dot_general(
        spread, listed_ref[...], (((1,), (1,)), ((), ())), preferred_element_type=F32
    )
    wgrads = [
        lax.dot_general(x[...], grad, (((1,), (1,)), ((), ())), preferred_element_type=F32)
        for x in (feat_ref, aggs[0])
    ]
    ones = jnp.ones((16, nodes), BF16)
    bias = lax.dot_general(
        ones, cot_full[own_rows, :].astype(BF16), (((1,), (1,)), ((), ())), preferred_element_type=F32
    )[:1]
    high = bias.astype(BF16).astype(F32)
    listed = listed_ref.shape[0] // nodes
    half, short = width // 2, width // LOW
    base = listed * short + half
    for q in range(LOW):
        for r in range(listed):
            wide[q, r * short : (r + 1) * short, :] = contrib[
                q * short : (q + 1) * short, r * nodes : (r + 1) * nodes
            ]
        wide[q, base - half : base, :] = wgrads[q // 2][q % 2 * half : (q % 2 + 1) * half, :]
        wide[q, base:, :] = jnp.zeros((wide.shape[1] - base, nodes), F32)
        wide[q, base : base + 1, :part_h] = high
        wide[q, base + 1 : base + 2, :part_h] = bias - high
    low = lax.axis_index("dom") % LOW
    for m in range(LOW):
        slots[m][...] = wide[jnp.bitwise_xor(low, m)].astype(BF16)


def group_sum_body(base, *refs):
    got, (out_ref, wide, full) = refs[:LOW], refs[LOW:]
    low = lax.axis_index("dom") % LOW
    for m in range(LOW):
        wide[jnp.bitwise_xor(low, m)] = got[m][...].astype(F32)
    total = wide[0] + wide[1] + wide[2] + wide[3]
    full[...] = total
    bias = total[base : base + 1] + total[base + 1 : base + 2]
    high = bias.astype(BF16).astype(F32)
    full[base : base + 1, :] = high
    full[base + 1 : base + 2, :] = bias - high
    out_ref[...] = full[...].astype(BF16)


def line_sum_body(base, width, count, pick_ref, *refs):
    got, bias_ref, outs = refs[:count], refs[count], refs[count + 1 : count + 1 + LOW]
    wide, piece, pieces = refs[count + 1 + LOW :]
    me = lax.axis_index("dom")
    place = me // LOW
    for m in range(count):
        wide[jnp.bitwise_xor(place, m)] = got[m][...].astype(F32)
    total = wide[0]
    for m in range(1, count):
        total += wide[m]
    bias_ref[...] = jnp.broadcast_to(total[base : base + 1] + total[base + 1 : base + 2], bias_ref.shape)
    half, short = width // 2, width // LOW
    piece[...] = jnp.zeros_like(piece)
    piece[short : short + half, :] = total[base - half : base]
    listed = pick_ref.shape[0] // LOW
    for q in range(LOW):
        mine = jnp.zeros((short, total.shape[1]), F32)
        for r in range(listed):
            row = q * listed + r
            mine += pick_ref[row : row + 1, :] * total[r * short : (r + 1) * short]
        piece[:short, :] = mine
        pieces[q] = piece[...]
    for m in range(LOW):
        outs[m][...] = pieces[jnp.bitwise_xor(me % LOW, m)].astype(BF16)


def last_body(scale_ref, act_ref, bias_ref, own_ref, *refs):
    got, (act_out, feat_ref, self_ref, nbr_ref, bias_out, wide, back) = refs[:LOW], refs[LOW:]
    act_out[...] = act_ref[...]
    bias_out[...] = bias_ref[:1, : bias_out.shape[1]]
    width = own_ref.shape[0]
    me = lax.axis_index("dom")
    low = me % LOW
    half, short = width // 2, width // LOW
    for m in range(LOW):
        wide[jnp.bitwise_xor(low, m)] = got[m][...].astype(F32)
    fresh = scale_ref[16:17, :]
    for q in range(LOW):
        back[q * short : (q + 1) * short, :] = wide[q, :short]
        ref = nbr_ref if q // 2 else self_ref
        ref[q % 2 * half : (q % 2 + 1) * half, :] = wide[q, short : short + half]
    feat_ref[...] = (own_ref[...] + fresh * back[...]).astype(BF16)


def per_device(
    n_col,
    features,
    cached_embed,
    staleness,
    node_counts,
    neighbours,
    degrees,
    w_self,
    w_nbr,
    sage_bias,
    cotangent,
):
    width, nodes = features.shape
    hidden = w_self.shape[1]
    dom = staleness.shape[0]
    listed = dom // 4
    part_h = cotangent.shape[0]
    shape = jax.ShapeDtypeStruct

    def hop(block, m):
        return lax.ppermute(block, "dom", [(i, i ^ m) for i in range(dom)])

    def along(block):
        far_first = [hop(block, m) for m in range(dom - LOW, 0, -LOW)]
        return [block] + far_first[::-1]

    def within(slots):
        return [slots[0]] + [hop(slots[m], m) for m in range(1, LOW)]

    def around(block):
        return [
            lax.ppermute(block, "col", [(i, (i + s) % n_col) for i in range(n_col)])
            for s in range(1, n_col)
        ]

    line = along(features)
    bias_row = sage_bias.reshape(1, part_h)
    packed = call(
        pack_body,
        shape((3 * width + part_h + 16, nodes), BF16),
        0,
        0,
        [pltpu.VMEM((1, part_h), F32), pltpu.VMEM((16, nodes), F32), pltpu.SemaphoreType.DMA((5,))],
        moved=4 * (3 * width + part_h) * nodes,
        hbm_count=5,
    )(features, w_self, w_nbr, cotangent, bias_row)
    packs = around(packed)
    deg = degrees.reshape(1, nodes)
    stacked = call(stack_body, shape((width * len(line), nodes), BF16), 0, len(line), moved=4 * dom * width * nodes // LOW)(
        *line
    )
    stacks = within([stacked] * LOW)
    counts, acc, scale, picks, finds = call(
        count_body,
        (
            shape((listed * nodes, nodes), BF16),
            shape((width, nodes), F32),
            shape((24, nodes), F32),
            shape((LOW * listed, nodes), F32),
            shape((dom * listed, nodes), F32),
        ),
        2,
        3,
        [pltpu.VMEM((dom * nodes, nodes), BF16), pltpu.SMEM((dom,), jnp.int32)],
        flops=2 * width * dom * nodes * nodes,
        moved=dom * nodes * nodes * 16,
    )(staleness, node_counts, neighbours, deg, cached_embed)
    agg = call(
        mean_body,
        shape((width, nodes), BF16),
        0,
        4 + LOW,
        moved=2 * dom * width * nodes,
    )(finds, scale, acc, counts, *stacks)
    aggs = [agg] + around(agg)
    base = listed * (width // LOW) + width // 2
    rows = up16(base + 2)
    act, own, *slots = call(
        functools.partial(dense_body, n_col),
        [shape((part_h, nodes), BF16), shape((width, nodes), F32)] + [shape((rows, nodes), BF16)] * LOW,
        0,
        7 + 2 * n_col - 1,
        [
            pltpu.VMEM((hidden, nodes), F32),
            pltpu.VMEM((hidden, LANES), F32),
            pltpu.VMEM((hidden, nodes), F32),
            pltpu.VMEM((LOW, rows, nodes), F32),
        ],
        flops=2 * width * nodes * (hidden * 6 + listed * nodes),
        moved=4 * LOW * rows * nodes,
    )(scale, counts, features, w_self, w_nbr, bias_row, cotangent, *aggs, *packs)
    summed = call(
        functools.partial(group_sum_body, base),
        shape((rows, nodes), BF16),
        0,
        LOW,
        [pltpu.VMEM((LOW, rows, nodes), F32), pltpu.VMEM((rows, nodes), F32)],
        moved=2 * LOW * rows * nodes,
    )(*within(slots))
    lines = along(summed)
    tall = up16(width // LOW + width // 2)
    bias, *pieces = call(
        functools.partial(line_sum_body, base, width, len(lines)),
        [shape((8, nodes), F32)] + [shape((tall, nodes), BF16)] * LOW,
        0,
        1 + len(lines),
        [
            pltpu.VMEM((len(lines), rows, nodes), F32),
            pltpu.VMEM((tall, nodes), F32),
            pltpu.VMEM((LOW, tall, nodes), F32),
        ],
        moved=2 * len(lines) * rows * nodes,
    )(picks, *lines)
    act, grad_feat, grad_self, grad_nbr, bias = call(
        last_body,
        (
            shape((part_h, nodes), BF16),
            shape((width, nodes), BF16),
            shape((width, hidden), F32),
            shape((width, hidden), F32),
            shape((1, part_h), F32),
        ),
        0,
        4 + LOW,
        [pltpu.VMEM((LOW, tall, nodes), F32), pltpu.VMEM((width, nodes), F32)],
        moved=2 * LOW * tall * nodes,
    )(scale, act, bias, own, *within(pieces))
    return act, grad_feat, grad_self, grad_nbr, bias.reshape(-1)


def solution(mesh):
    placed = (
        P("col", "dom"),
        P("col", None),
        P(),
        P(),
        P(None, "dom"),
        P("dom"),
        P("col", None),
        P("col", None),
        P("col"),
        P("col", "dom"),
    )
    return jax.shard_map(
        functools.partial(per_device, mesh.shape["col"]),
        mesh=mesh,
        in_specs=placed,
        out_specs=(P("col", "dom"), P("col", "dom"), P("col", None), P("col", None), P("col")),
        check_vma=False,
    )
```
